32 devices in a mesh: rep: 8 (over y, x, core), head: 4 (over z).
Axes of the slice: x: 2, y: 2, z: 4, core: 2. Of those that a mesh axis runs over, the one named last changes fastest.
Arguments:
- ssd_x: bfloat16 [512, 4096], P('rep', 'head'), may hold values from -6 to 6
- gate_z: bfloat16 [512, 4096], P('rep', 'head'), may hold values from -6 to 6
- group_b: bfloat16 [512, 512], P('rep', 'head'), may hold values from -6 to 6
- group_c: bfloat16 [512, 512], P('rep', 'head'), may hold values from -0.5 to 0.5
- step_dt: bfloat16 [512, 64], P('rep', 'head'), may hold values from 0.5 to 2
- queries: bfloat16 [512, 4096], P('rep', 'head'), may hold values from -8 to 8
- tail_kv: bfloat16 [512, 1024], P('rep', 'head'), may hold values from -6 to 6
- ckpt_state: bfloat16 [32, 64, 64, 128], P('rep', 'head'), may hold values from -6 to 6
- kv_pool: bfloat16 [512, 16, 1024], P('rep', None, 'head'), may hold values from -8 to 8
- w_out: bfloat16 [4096, 4096], P('head', 'rep'), may hold values from -0.125 to 0.125
- decay_rate: float32 [64], P('head'), may hold values from 0.002 to 2
- skip_d: float32 [64], P('head'), may hold values from 0.5 to 1.5
- norm_gain: float32 [4096], P('head'), may hold values from 0.5 to 1.5
- owner: int32 [32], replicated, may hold values from 0 to 7, as said below
- slot: int32 [32], replicated, may hold values from 0 to 3, as said below
- page_table: int32 [32, 16], replicated, may hold values from 0 to 63, as said below
- hit_len: int32 [32], replicated, may hold values from 2 to 256, as said below
- tail_len: int32 [32], replicated, may hold values from 1 to 16, as said below
Outputs:
- ssd_out: bfloat16 [512, 4096], P('rep', 'head')
- attn_proj: bfloat16 [512, 4096], P('rep', 'head')
- final_state: bfloat16 [32, 64, 64, 128], P('rep', 'head')
The draws below stay inside these ranges and needn't reach their ends.
Inputs may be any that keep to these rules, and one draw needn't show every extreme that they name: Every replica owns exactly 4 requests, and no two requests of one replica share an owner. `slot`: the requests of one owner have distinct slots. `page_table`: each of an owner's 64 pages belongs to exactly one of its requests. `hit_len`: some request has exactly 256. `tail_len`: some request has exactly 16.
All inputs are finite; a program needn't handle non-finite values.
Results may differ from the reference program's by a relative error of at most 0.0057.
Values may be sent and summed in bfloat16 or wider, within the bound.
A program may use at most 192 MiB of HBM per device.

```python
import math
import jax
import jax.numpy as jnp
from jax import lax

REQ_DEV = 4
TAIL = 16
CACHE = 256
PAGE = 16
SSD_DEV = 16
HEAD_DIM = 64
STATE = 128
QH_DEV = 8
DH = 128
D_OUT = 4096
REQS = 32
TOKENS = 512
PAGES_REQ = 16
POOL_DEV = 64
POOL = 512
SSD_HEADS = 64
QHEADS = 32
KV_WIDTH = 1024
N_REP = 8
N_HEAD = 4


def choose_owners(key):
    base = jax.random.fold_in(key, 11)
    first_key, second_key, third_key, fourth_key = jax.random.split(base, 4)
    replicas = REQS // REQ_DEV
    order = jax.random.permutation(first_key, replicas)
    places = jax.random.permutation(second_key, replicas)
    shifts = jax.random.permutation(third_key, replicas)[:REQ_DEV]
    owners = order[(places[:, None] + shifts[None, :]) % replicas]
    scores = jax.random.randint(fourth_key, (replicas, REQ_DEV), 0, 1 << 16) * REQ_DEV + jnp.arange(REQ_DEV)[None, :]
    ranking = jnp.argsort(scores, axis=1)
    slot_ids = ranking[owners, jnp.arange(REQ_DEV)[None, :]]
    return (owners.reshape(-1).astype(jnp.int32), slot_ids.reshape(-1).astype(jnp.int32))


def draw_owner(key, part):
    return choose_owners(key)[0]


def draw_slot(key, part):
    return choose_owners(key)[1]


def draw_page_table(key, part):
    owners, slot_ids = choose_owners(key)
    replicas = REQS // REQ_DEV
    scores = jax.random.randint(jax.random.fold_in(key, 13), (replicas, POOL_DEV), 0, 1 << 16) * POOL_DEV + jnp.arange(POOL_DEV)[None, :]
    ranking = jnp.argsort(scores, axis=1)
    columns = slot_ids[:, None] * PAGES_REQ + jnp.arange(PAGES_REQ)[None, :]
    return ranking[owners[:, None], columns].astype(jnp.int32)


def draw_hit_len(key, part):
    values = jax.random.randint(jax.random.fold_in(key, 17), (REQS,), 2, CACHE + 1)
    chosen = jax.random.randint(jax.random.fold_in(key, 19), (), 0, REQS)
    return values.at[chosen].set(CACHE).astype(jnp.int32)


def draw_tail_len(key, part):
    values = jax.random.randint(jax.random.fold_in(key, 23), (REQS,), 1, TAIL + 1)
    chosen = jax.random.randint(jax.random.fold_in(key, 29), (), 0, REQS)
    return values.at[chosen].set(TAIL).astype(jnp.int32)


def draw_queries(key, part):
    inner_key = jax.random.fold_in(key, 37)
    shape = (TOKENS, QHEADS * DH)
    values = jax.random.truncated_normal(inner_key, -8.0, 8.0, shape, jnp.float32)
    return values.astype(jnp.bfloat16)


def draw_kv_pool(key, part):
    inner_key = jax.random.fold_in(key, 41)
    shape = (POOL, PAGE, KV_WIDTH)
    values = jax.random.truncated_normal(inner_key, -8.0, 8.0, shape, jnp.float32)
    return values.astype(jnp.bfloat16)


def spiked(values, stream_key, source, target, shards_of, factor):
    owner, partner = [(jnp.arange(values.shape[dim]) // (values.shape[dim] // shards_of)).reshape([-1 if axis == dim else 1 for axis in range(values.ndim)]) for dim in (source, target)]
    chosen = jax.random.permutation(stream_key, shards_of)[partner]
    strong = (owner == chosen) | (owner == (partner + shards_of // 2) % shards_of)
    return jnp.where(strong, factor * values, values)


def levels(key, shape, cuts, least, high):
    def one(axis_at, shards_of):
        draws = jax.random.uniform(jax.random.fold_in(jax.random.fold_in(key, 6), axis_at), (shards_of,), jnp.float32, least / len(cuts), high / len(cuts))
        return jnp.repeat(jnp.exp(draws), shape[axis_at] // shards_of).reshape((-1,) + (1,) * (len(shape) - axis_at - 1))

    factor_of = one(*cuts[0])
    for cut in cuts[1:]:
        factor_of = factor_of * one(*cut)
    return factor_of


def normal_values(stream_key, shape, deviation, limit, shards=(), kind=jnp.bfloat16):
    values = jax.random.normal(stream_key, shape, jnp.float32) * deviation
    if len(shards) > 0:
        values = levels(stream_key, shape, shards, -0.22, 0.18) * values
    return jnp.clip(values, min=-limit, max=limit).astype(kind)


def bell_draw_with(own_key, extent, scale, bound, cuts, heavy, held_as=jnp.bfloat16):
    values = scale * jax.random.normal(own_key, extent, jnp.float32)
    if cuts:
        values = values * levels(own_key, extent, cuts, -0.22, 0.18)
    return jnp.clip(spiked(values, jax.random.fold_in(own_key, 3), *heavy), -bound, bound).astype(held_as)


def setup_inputs(seed: int = 0) -> dict:
    keys = jax.random.split(jax.random.key(seed), 19)
    ssd_x = normal_values(keys[0], (TOKENS, SSD_HEADS * HEAD_DIM), 1.0, 6.0, ((0, 8), (1, 4)))
    gate_z = normal_values(keys[1], (TOKENS, SSD_HEADS * HEAD_DIM), 1.0, 6.0, ((0, 8), (1, 4)))
    group_b = normal_values(keys[2], (TOKENS, STATE * N_HEAD), 1.0, 6.0, ((0, 8), (1, 4)))
    group_c = normal_values(keys[3], (TOKENS, STATE * N_HEAD), STATE ** -0.5, 0.5, ((0, 8), (1, 4)))
    step_dt = jnp.clip(jnp.exp(math.log(2.0) - 1.3862944 * jax.random.uniform(keys[4], (TOKENS, SSD_HEADS), jnp.float32) ** levels(keys[4], (TOKENS, SSD_HEADS), ((0, 8), (1, 4)), -0.2, 0.2)), 0.5, 2.0).astype(jnp.bfloat16)
    queries = draw_queries(jax.random.fold_in(keys[18], 71), 0)
    tail_kv = normal_values(keys[6], (TOKENS, KV_WIDTH), 1.0, 6.0, ((0, 8), (1, 4)))
    ckpt_state = normal_values(keys[7], (REQS, SSD_HEADS, HEAD_DIM, STATE), 1.0, 6.0, ((0, 8), (1, 4)))
    kv_pool = draw_kv_pool(jax.random.fold_in(keys[18], 71), 0)
    w_out = bell_draw_with(keys[9], (QHEADS * DH, D_OUT), (QHEADS * DH) ** -0.5, 0.125, ((0, 4), (1, 8)), (0, 1, 8, 2.0))
    decay_rate = jnp.clip(jnp.exp(math.log(2.0) - 6.9077552 * jax.random.uniform(keys[10], (SSD_HEADS,), jnp.float32) ** levels(keys[10], (SSD_HEADS,), ((0, 4),), -0.2, 0.2)), 0.002, 2.0)
    skip_d = jnp.clip(0.5 + 1.0 * jax.random.uniform(keys[11], (SSD_HEADS,), jnp.float32) ** levels(keys[11], (SSD_HEADS,), ((0, 4),), -0.2, 0.2), 0.5, 1.5)
    norm_gain = jnp.clip(1.0 + 0.1 * jax.random.normal(keys[12], (SSD_HEADS * HEAD_DIM,), jnp.float32), 0.5, 1.5)
    owner = draw_owner(jax.random.fold_in(keys[18], 71), 0)
    slot = draw_slot(jax.random.fold_in(keys[18], 71), 0)
    page_table = draw_page_table(jax.random.fold_in(keys[18], 71), 0)
    hit_len = draw_hit_len(jax.random.fold_in(keys[18], 71), 0)
    tail_len = draw_tail_len(jax.random.fold_in(keys[18], 71), 0)
    return {"ssd_x": ssd_x, "gate_z": gate_z, "group_b": group_b, "group_c": group_c, "step_dt": step_dt, "queries": queries, "tail_kv": tail_kv, "ckpt_state": ckpt_state, "kv_pool": kv_pool, "w_out": w_out, "decay_rate": decay_rate, "skip_d": skip_d, "norm_gain": norm_gain, "owner": owner, "slot": slot, "page_table": page_table, "hit_len": hit_len, "tail_len": tail_len}


highest = lax.Precision.HIGHEST

def scan_heads(signal, b_rows, c_rows, step_sizes, state_start, rates, skipping, alive):
    length = signal.shape[1]
    head_count = signal.shape[2]
    fanout = head_count // b_rows.shape[2]
    log_decay = -rates[None, None, :] * step_sizes * alive[:, :, None]
    running = jnp.cumsum(log_decay, axis=1)
    position = jnp.arange(length, dtype=jnp.int32)
    causal = (position[:, None] >= position[None, :])[None, :, :, None]
    spans = running[:, :, None, :] - running[:, None, :, :]
    decays = jnp.where(causal, jnp.exp(jnp.where(causal, spans, 0.0)), 0.0)
    intersection = jnp.einsum('ktgn,kugn->ktug', c_rows, b_rows, precision=highest)
    intersection_head = jnp.repeat(intersection, fanout, axis=3)
    weighted_dt = step_sizes * alive[:, :, None]
    mixing = decays * intersection_head * weighted_dt[:, None, :, :]
    within = jnp.einsum('ktue,kuep->ktep', mixing, signal, precision=highest)
    c_heads = jnp.repeat(c_rows, fanout, axis=2)
    b_heads = jnp.repeat(b_rows, fanout, axis=2)
    from_state = jnp.exp(running)[..., None] * jnp.einsum('kten,kepn->ktep', c_heads, state_start, precision=highest)
    mixer = (within + from_state + skipping[None, None, :, None] * signal) * alive[:, :, None, None]
    last_cum = running[:, -1, :]
    weights_in = jnp.exp(last_cum[:, None, :] - running) * weighted_dt
    closing = jnp.exp(last_cum)[:, :, None, None] * state_start + jnp.einsum('kue,kuen,kuep->kepn', weights_in, b_heads, signal, precision=highest)
    return (mixer, closing)

def attend(query_rows, cached, tail_rows, hit_sizes, tail_sizes, alive):
    batch = query_rows.shape[0]
    query_len = query_rows.shape[1]
    cache_len = cached.shape[1]
    scaling = 1.0 / math.sqrt(query_rows.shape[-1])
    cached_scores = jnp.einsum('ktaqd,kcad->ktaqc', query_rows, cached[:, :, :, 0, :], precision=highest) * scaling
    tail_scores = jnp.einsum('ktaqd,kuad->ktaqu', query_rows, tail_rows[:, :, :, 0, :], precision=highest) * scaling
    positions = jnp.arange(cache_len, dtype=jnp.int32)
    position = jnp.arange(query_len, dtype=jnp.int32)
    seen_cache = jnp.broadcast_to((positions[None, :] < hit_sizes[:, None])[:, None, :], (batch, query_len, cache_len))
    seen_tail = (position[None, None, :] <= position[None, :, None]) & (position[None, None, :] < tail_sizes[:, None, None])
    visible = jnp.concatenate([seen_cache, seen_tail], axis=2)[:, :, None, None, :]
    scores = jnp.where(visible, jnp.concatenate([cached_scores, tail_scores], axis=4), -1e+30)
    row_max = lax.optimization_barrier(jnp.max(scores, axis=4, keepdims=True))
    exponent = jnp.where(visible, jnp.exp(scores - row_max), 0.0)
    weights = (exponent / lax.optimization_barrier(jnp.sum(exponent, axis=4, keepdims=True))).astype(jnp.bfloat16).astype(jnp.float32)
    result = jnp.einsum('ktaqc,kcad->ktaqd', weights[..., :cache_len], cached[:, :, :, 1, :], precision=highest)
    result = result + jnp.einsum('ktaqu,kuad->ktaqd', weights[..., cache_len:], tail_rows[:, :, :, 1, :], precision=highest)
    return (result * alive[:, :, None, None, None]).astype(jnp.bfloat16)

def reference(ssd_x, gate_z, group_b, group_c, step_dt, queries, tail_kv, ckpt_state, kv_pool, w_out, decay_rate, skip_d, norm_gain, owner, slot, page_table, hit_len, tail_len):
    channels = SSD_HEADS * HEAD_DIM
    group_width = SSD_DEV * HEAD_DIM

    def one_home(home):
        first_row = home * REQ_DEV
        request_ids = first_row + jnp.arange(REQ_DEV, dtype=jnp.int32)
        owners = owner[request_ids]
        slot_ids = slot[request_ids]
        hit_sizes = hit_len[request_ids]
        tail_sizes = tail_len[request_ids]
        state_start = ckpt_state[owners * REQ_DEV + slot_ids].astype(jnp.float32)
        page_rows = kv_pool[owners[:, None] * POOL_DEV + page_table[request_ids]]
        cached = page_rows.reshape(REQ_DEV, CACHE, N_HEAD, 2, DH).astype(jnp.float32)

        def per_request(array):
            block = lax.dynamic_slice_in_dim(array, (first_row * TAIL).astype(jnp.int32), REQ_DEV * TAIL, 0)
            return block.reshape(REQ_DEV, TAIL, -1)
        alive = (jnp.arange(TAIL, dtype=jnp.int32)[None, :] < tail_sizes[:, None]).astype(jnp.float32)
        signal = per_request(ssd_x).reshape(REQ_DEV, TAIL, SSD_HEADS, HEAD_DIM).astype(jnp.float32)
        b_rows = per_request(group_b).reshape(REQ_DEV, TAIL, N_HEAD, STATE).astype(jnp.float32)
        c_rows = per_request(group_c).reshape(REQ_DEV, TAIL, N_HEAD, STATE).astype(jnp.float32)
        step_sizes = per_request(step_dt).astype(jnp.float32)
        mixer, closing = scan_heads(signal, b_rows, c_rows, step_sizes, state_start, decay_rate, skip_d, alive)
        gate_rows = per_request(gate_z).reshape(REQ_DEV, TAIL, SSD_HEADS, HEAD_DIM).astype(jnp.float32)
        gated_out = (mixer * jax.nn.silu(gate_rows)).reshape(REQ_DEV, TAIL, N_HEAD, group_width)
        energy = lax.optimization_barrier(jnp.sum(gated_out * gated_out, axis=3, keepdims=True))
        normed = gated_out / jnp.sqrt(energy / group_width + 1e-05) * norm_gain.reshape(N_HEAD, group_width)
        query_rows = per_request(queries).reshape(REQ_DEV, TAIL, N_HEAD, QH_DEV, DH).astype(jnp.float32)
        tail_rows = per_request(tail_kv).reshape(REQ_DEV, TAIL, N_HEAD, 2, DH).astype(jnp.float32)
        attention = attend(query_rows, cached, tail_rows, hit_sizes, tail_sizes, alive)
        projected = jnp.dot(attention.reshape(REQ_DEV * TAIL, QHEADS * DH), w_out, preferred_element_type=jnp.float32)
        return (normed.astype(jnp.bfloat16).reshape(REQ_DEV * TAIL, channels), projected.astype(jnp.bfloat16), closing.astype(jnp.bfloat16))
    gathered = lax.map(one_home, jnp.arange(N_REP, dtype=jnp.int32))
    return (gathered[0].reshape(TOKENS, SSD_HEADS * HEAD_DIM), gathered[1].reshape(TOKENS, D_OUT), gathered[2].reshape(REQS, SSD_HEADS, HEAD_DIM, STATE))
```

```python
import functools
import math

import jax
import jax.numpy as jnp
from jax import lax
from jax.experimental import pallas as pl
from jax.experimental.pallas import tpu as pltpu
from jax.sharding import PartitionSpec as P

TAIL = 16
STATE = 128
QH_DEV = 8
DH = 128


highest = lax.Precision.HIGHEST


def scan_heads(signal, b_rows, c_rows, step_sizes, state_start, rates, skipping, alive):
    length = signal.shape[1]
    head_count = signal.shape[2]
    fanout = head_count // b_rows.shape[2]
    log_decay = -rates[None, None, :] * step_sizes * alive[:, :, None]
    running = jnp.cumsum(log_decay, axis=1)
    position = jnp.arange(length, dtype=jnp.int32)
    causal = (position[:, None] >= position[None, :])[None, :, :, None]
    spans = running[:, :, None, :] - running[:, None, :, :]
    decays = jnp.where(causal, jnp.exp(jnp.where(causal, spans, 0.0)), 0.0)
    intersection = jnp.einsum("ktgn,kugn->ktug", c_rows, b_rows, precision=highest)
    intersection_head = jnp.repeat(intersection, fanout, axis=3)
    weighted_dt = step_sizes * alive[:, :, None]
    mixing = decays * intersection_head * weighted_dt[:, None, :, :]
    within = jnp.einsum("ktue,kuep->ktep", mixing, signal, precision=highest)
    c_heads = jnp.repeat(c_rows, fanout, axis=2)
    b_heads = jnp.repeat(b_rows, fanout, axis=2)
    from_state = jnp.exp(running)[..., None] * jnp.einsum(
        "kten,kepn->ktep", c_heads, state_start, precision=highest
    )
    mixer = (within + from_state + skipping[None, None, :, None] * signal) * alive[:, :, None, None]
    last_cum = running[:, -1, :]
    weights_in = jnp.exp(last_cum[:, None, :] - running) * weighted_dt
    closing = jnp.exp(last_cum)[:, :, None, None] * state_start + jnp.einsum(
        "kue,kuen,kuep->kepn", weights_in, b_heads, signal, precision=highest
    )
    return (mixer, closing)


def attend(query_rows, cached, tail_rows, hit_sizes, tail_sizes, alive):
    batch = query_rows.shape[0]
    query_len = query_rows.shape[1]
    cache_len = cached.shape[1]
    scaling = 1.0 / math.sqrt(query_rows.shape[-1])
    cached_scores = (
        jnp.einsum(
            "ktaqd,kcad->ktaqc",
            query_rows,
            cached[:, :, :, 0, :],
            preferred_element_type=jnp.float32,
        )
        * scaling
    )
    tail_scores = (
        jnp.einsum(
            "ktaqd,kuad->ktaqu",
            query_rows,
            tail_rows[:, :, :, 0, :],
            preferred_element_type=jnp.float32,
        )
        * scaling
    )
    positions = jnp.arange(cache_len, dtype=jnp.int32)
    position = jnp.arange(query_len, dtype=jnp.int32)
    seen_cache = jnp.broadcast_to(
        (positions[None, :] < hit_sizes[:, None])[:, None, :], (batch, query_len, cache_len)
    )
    seen_tail = (position[None, None, :] <= position[None, :, None]) & (
        position[None, None, :] < tail_sizes[:, None, None]
    )
    visible = jnp.concatenate([seen_cache, seen_tail], axis=2)[:, :, None, None, :]
    scores = jnp.where(visible, jnp.concatenate([cached_scores, tail_scores], axis=4), -1e30)
    row_max = jnp.max(scores, axis=4, keepdims=True)
    exponent = jnp.where(visible, jnp.exp(scores - row_max), 0.0)
    weights = (exponent / jnp.sum(exponent, axis=4, keepdims=True)).astype(jnp.bfloat16)
    result = jnp.einsum(
        "ktaqc,kcad->ktaqd",
        weights[..., :cache_len],
        cached[:, :, :, 1, :],
        preferred_element_type=jnp.float32,
    )
    result = result + jnp.einsum(
        "ktaqu,kuad->ktaqd",
        weights[..., cache_len:],
        tail_rows[:, :, :, 1, :],
        preferred_element_type=jnp.float32,
    )
    return (result * alive[:, :, None, None, None]).astype(jnp.bfloat16)


def spread(selector, values):
    flat = values.reshape(values.shape[0], -1)
    mixed = jnp.dot(selector, flat, preferred_element_type=jnp.float32)
    return mixed.astype(values.dtype).reshape((selector.shape[0],) + values.shape[1:])


def local(
    ssd_x,
    gate_z,
    group_b,
    group_c,
    step_dt,
    queries,
    tail_kv,
    ckpt_state,
    kv_pool,
    w_out,
    decay_rate,
    skip_d,
    norm_gain,
    owner,
    slot,
    page_table,
    hit_len,
    tail_len,
):
    replicas = lax.axis_size("rep")
    myself = lax.axis_index("rep")
    slot_count = ckpt_state.shape[0]
    head_count = ckpt_state.shape[1]
    head_size = ckpt_state.shape[2]
    group_width = head_count * head_size
    kv_columns = tail_kv.shape[1]
    kv_heads = kv_columns // (2 * DH)
    homes = jnp.arange(replicas, dtype=jnp.int32)
    slot_range = jnp.arange(slot_count, dtype=jnp.int32)
    owner_grid = owner.reshape(replicas, slot_count)
    slot_grid = slot.reshape(replicas, slot_count)
    hit_grid = hit_len.reshape(replicas, slot_count)
    tail_grid = tail_len.reshape(replicas, slot_count)
    page_grid = page_table.reshape(replicas, slot_count, -1)
    is_mine = (homes == myself)[:, None]
    my_owner = jnp.sum(jnp.where(is_mine, owner_grid, 0), axis=0)
    my_hit = jnp.sum(jnp.where(is_mine, hit_grid, 0), axis=0)
    my_tail = jnp.sum(jnp.where(is_mine, tail_grid, 0), axis=0)
    to_owner = (homes[:, None] == my_owner[None, :]).astype(jnp.bfloat16)
    holding = (
        (owner_grid == myself)[:, :, None] & (slot_grid[:, :, None] == slot_range[None, None, :])
    ).astype(jnp.int32)
    slot_home = jnp.sum(holding, axis=1).T.astype(jnp.bfloat16)
    slot_pages = jnp.sum(holding[:, :, :, None] * page_grid[:, :, None, :], axis=(0, 1))
    pool_range = jnp.arange(kv_pool.shape[0], dtype=jnp.int32)
    page_pick = (slot_pages.reshape(-1, 1) == pool_range[None, :]).astype(jnp.bfloat16)
    cache_own = spread(page_pick, kv_pool).reshape(slot_count, -1, kv_columns)

    def per_request(array):
        return array.reshape(slot_count, TAIL, -1)

    home_pick = slot_home.T
    fetched = (
        lax.all_to_all(
            spread(home_pick, ckpt_state), "rep", split_axis=0, concat_axis=0, tiled=True
        ),
        lax.all_to_all(
            spread(home_pick, cache_own), "rep", split_axis=0, concat_axis=0, tiled=True
        ),
    )
    owner_pick = to_owner.T
    state_start = spread(owner_pick, fetched[0])
    cached = spread(owner_pick, fetched[1])
    signal_in = per_request(ssd_x)
    batch = signal_in.shape[0]
    alive = (jnp.arange(TAIL, dtype=jnp.int32)[None, :] < my_tail[:, None]).astype(jnp.float32)
    signal = signal_in.reshape(batch, TAIL, head_count, head_size).astype(jnp.float32)
    b_rows = per_request(group_b).reshape(batch, TAIL, -1, STATE).astype(jnp.float32)
    c_rows = per_request(group_c).reshape(batch, TAIL, -1, STATE).astype(jnp.float32)
    mixer, closing = scan_heads(
        signal,
        b_rows,
        c_rows,
        per_request(step_dt).astype(jnp.float32),
        state_start.astype(jnp.float32),
        decay_rate,
        skip_d,
        alive,
    )
    gated_out = mixer * jax.nn.silu(
        per_request(gate_z).reshape(batch, TAIL, head_count, head_size).astype(jnp.float32)
    )
    energy = jnp.sum(gated_out * gated_out, axis=(2, 3))
    normed = (
        gated_out
        / jnp.sqrt(energy / group_width + 1e-05)[:, :, None, None]
        * norm_gain.reshape(head_count, head_size)
    )
    query_rows = per_request(queries).reshape(batch, TAIL, kv_heads, QH_DEV, DH)
    cached_rows = cached.reshape(batch, -1, kv_heads, 2, DH)
    tail_rows = per_request(tail_kv).reshape(batch, TAIL, kv_heads, 2, DH)
    attention = attend(query_rows, cached_rows, tail_rows, my_hit, my_tail, alive)
    ssd_rows = normed.astype(jnp.bfloat16).reshape(batch, TAIL, -1)
    attn_rows = attention.reshape(batch, TAIL, -1)
    final_rows = closing.astype(jnp.bfloat16)
    attn_flat = attn_rows.reshape(slot_count * TAIL, -1)
    terms = jnp.dot(
        attn_flat,
        lax.all_gather(w_out, "rep", axis=1, tiled=True),
        preferred_element_type=jnp.float32,
    )
    projected = lax.psum_scatter(terms, "head", scatter_dimension=1, tiled=True).astype(
        jnp.bfloat16
    )
    return (ssd_rows.reshape(slot_count * TAIL, -1), projected, final_rows)


MESH = pl.DeviceIdType.MESH
VMEM_BUDGET = 24 * 2**20


def dot(a, b, dims=((1,), (0,)), precision=None):
    return lax.dot_general(
        a, b, (dims, ((), ())), precision=precision, preferred_element_type=jnp.float32
    )


def layer(
    n,
    m,
    owner,
    slot,
    page,
    hit,
    tail,
    x,
    z,
    b,
    c,
    dt,
    q,
    tkv,
    ckpt,
    pool,
    w,
    rate,
    skip,
    gain,
    ssd_o,
    proj_o,
    fin_o,
    kv_out,
    kv_in,
    st_out,
    st_in,
    rows_all,
    part,
    shares,
    sums,
    cum_s,
    xw_s,
    log_s,
    acc_s,
    kv_ss,
    kv_rs,
    st_ss,
    st_rs,
    rows_ss,
    rows_rs,
    part_ss,
    part_rs,
    sum_ss,
    sum_rs,
):
    me = lax.axis_index("rep")
    hd = lax.axis_index("head")
    reqs = ckpt.shape[0]
    heads = ckpt.shape[1]
    size = ckpt.shape[2]
    width = heads * size
    pages = page.shape[1]
    cache = pages * pool.shape[1]
    span = n // m

    def to_rep(s):
        return lax.rem(me + s, n)

    def from_rep(s):
        return lax.rem(me + n - s, n)

    barrier = pltpu.get_barrier_semaphore()
    for s in range(1, n):
        pl.semaphore_signal(
            barrier, inc=1, device_id={"rep": to_rep(s)}, device_id_type=MESH
        )
    for u in range(1, m):
        pl.semaphore_signal(
            barrier, inc=1, device_id={"head": lax.rem(hd + u, m)}, device_id_type=MESH
        )

    def kv_copy(s):
        return pltpu.make_async_remote_copy(
            src_ref=kv_out.at[s],
            dst_ref=kv_in.at[s],
            send_sem=kv_ss.at[s],
            recv_sem=kv_rs.at[s],
            device_id={"rep": to_rep(s)},
            device_id_type=MESH,
        )

    def st_copy(s):
        return pltpu.make_async_remote_copy(
            src_ref=st_out.at[s],
            dst_ref=st_in.at[s],
            send_sem=st_ss.at[s],
            recv_sem=st_rs.at[s],
            device_id={"rep": to_rep(s)},
            device_id_type=MESH,
        )

    def rows_copy(s):
        return pltpu.make_async_remote_copy(
            src_ref=rows_all.at[0],
            dst_ref=rows_all.at[s],
            send_sem=rows_ss.at[s],
            recv_sem=rows_rs.at[s],
            device_id={"rep": to_rep(s)},
            device_id_type=MESH,
        )

    def part_copy(s):
        return pltpu.make_async_remote_copy(
            src_ref=part.at[s],
            dst_ref=shares.at[me],
            send_sem=part_ss.at[s],
            recv_sem=part_rs.at[s],
            device_id={"rep": from_rep(s)},
            device_id_type=MESH,
        )

    def sum_copy(u):
        to = lax.rem(hd + u, m)
        return pltpu.make_async_remote_copy(
            src_ref=shares.at[pl.ds(to * span, span)],
            dst_ref=sums.at[u],
            send_sem=sum_ss.at[u],
            recv_sem=sum_rs.at[u],
            device_id={"head": to},
            device_id_type=MESH,
        )

    def wanted(j):
        request = j * reqs
        for k in range(1, reqs):
            request = jnp.where(owner[j * reqs + k] == me, j * reqs + k, request)
        return request

    def pack_pages(s, target):
        request = wanted(to_rep(s))

        def one(i, carry):
            target[s, i] = pool[page[request, i]]
            return carry

        lax.fori_loop(0, pages, one, 0)

    for s in range(1, n):
        pack_pages(s, kv_out)
        if s == 1:
            pl.semaphore_wait(barrier, n - 1 + m - 1)
        kv_copy(s).start()
    pack_pages(0, kv_in)

    def pack_state(s, target):
        place = slot[wanted(to_rep(s))]

        def one(e, carry):
            target[s, e] = ckpt[place, e]
            return carry

        lax.fori_loop(0, heads, one, 0)

    for s in range(1, n):
        pack_state(s, st_out)
        st_copy(s).start()
    pack_state(0, st_in)

    lane = lax.broadcasted_iota(jnp.int32, (heads, width), 1)
    widen = (lane // size == lax.broadcasted_iota(jnp.int32, (heads, width), 0)).astype(
        jnp.float32
    )
    count = reqs * TAIL
    row = lax.broadcasted_iota(jnp.int32, (count, heads), 0)
    live = jnp.zeros((count, heads), jnp.float32)
    for k in range(reqs):
        first = k * TAIL
        live = jnp.where((row >= first) & (row < first + tail[me * reqs + k]), 1.0, live)
    weighted = dt[...].astype(jnp.float32) * live
    log_decay = -rate[...] * weighted
    log_s[...] = log_decay
    one_row = lax.broadcasted_iota(jnp.int32, (count, count), 0)
    one_col = lax.broadcasted_iota(jnp.int32, (count, count), 1)
    before = ((one_row >= one_col) & (one_row // TAIL == one_col // TAIL)).astype(jnp.float32)
    cum = dot(before, log_decay, precision=highest)
    cum_s[...] = dot(cum, widen, precision=highest)
    xw_s[...] = dot(weighted, widen, precision=highest) * x[...].astype(jnp.float32)
    skip_wide = dot(skip[...], widen, precision=highest)
    step = lax.broadcasted_iota(jnp.int32, (TAIL, 1), 0)

    def within(k, carry):
        rows = pl.ds(pl.multiple_of(k * TAIL, TAIL), TAIL)
        meet = dot(c[rows, :], b[rows, :], ((1,), (1,)))
        running = cum_s[rows, :]
        fed = xw_s[rows, :]
        total = skip_wide * x[rows, :].astype(jnp.float32)
        for u in range(TAIL):
            seen = step >= u
            decay = jnp.exp(jnp.where(seen, running - running[u : u + 1, :], 0.0))
            factor = jnp.where(seen, meet[:, u : u + 1], 0.0)
            total = total + decay * factor * fed[u : u + 1, :]
        acc_s[rows, :] = total
        return carry

    lax.fori_loop(0, reqs, within, 0)

    for s in range(1, n):
        kv_copy(s).wait_recv()

    scaling = 1.0 / math.sqrt(DH)

    def attention(k, carry):
        rows = pl.ds(pl.multiple_of(k * TAIL, TAIL), TAIL)
        request = me * reqs + k
        held = kv_in[lax.rem(me + n - owner[request], n)].reshape(cache, 2 * DH)
        fresh = tkv[rows, :]
        asked = jnp.concatenate(
            [q[rows, a * DH : (a + 1) * DH] for a in range(QH_DEV)], axis=0
        )
        far = dot(asked, held[:, :DH], ((1,), (1,))) * scaling
        near = dot(asked, fresh[:, :DH], ((1,), (1,))) * scaling
        place = lax.broadcasted_iota(jnp.int32, far.shape, 1)
        far_seen = place < hit[request]
        at = lax.rem(lax.broadcasted_iota(jnp.int32, near.shape, 0), TAIL)
        behind = lax.broadcasted_iota(jnp.int32, near.shape, 1)
        near_seen = (behind <= at) & (behind < tail[request])
        far = jnp.where(far_seen, far, -1e30)
        near = jnp.where(near_seen, near, -1e30)
        top = jnp.maximum(
            jnp.max(far, axis=1, keepdims=True), jnp.max(near, axis=1, keepdims=True)
        )
        far = jnp.where(far_seen, jnp.exp(far - top), 0.0)
        near = jnp.where(near_seen, jnp.exp(near - top), 0.0)
        whole = jnp.sum(far, axis=1, keepdims=True) + jnp.sum(near, axis=1, keepdims=True)
        far = (far / whole).astype(jnp.bfloat16)
        near = (near / whole).astype(jnp.bfloat16)
        result = dot(far, held[:, DH:]) + dot(near, fresh[:, DH:])
        result = jnp.concatenate(
            [result[a * TAIL : (a + 1) * TAIL, :] for a in range(QH_DEV)], axis=1
        )
        alive = (step < tail[request]).astype(jnp.float32)
        rows_all[0, rows, :] = (result * alive).astype(jnp.bfloat16)
        return carry

    lax.fori_loop(0, reqs, attention, 0)
    for s in range(1, n):
        rows_copy(s).start()

    for s in range(1, n):
        st_copy(s).wait_recv()

    def recur(k, carry):
        rows = pl.ds(pl.multiple_of(k * TAIL, TAIL), TAIL)
        request = me * reqs + k
        start = st_in[lax.rem(me + n - owner[request], n)]
        running = cum_s[rows, :]
        carried = dot(c[rows, :], start.reshape(width, start.shape[2]), ((1,), (1,)))
        alive = (step < tail[request]).astype(jnp.float32)
        mixer = (acc_s[rows, :] + jnp.exp(running) * carried) * alive
        gate = z[rows, :].astype(jnp.float32)
        gated = mixer * (gate / (1.0 + jnp.exp(-gate)))
        energy = jnp.sum(gated * gated, axis=1, keepdims=True)
        normed = gated / jnp.sqrt(energy / width + 1e-05) * gain[...]
        ssd_o[rows, :] = normed.astype(jnp.bfloat16)
        fed = jnp.exp(running[TAIL - 1 : TAIL, :] - running) * xw_s[rows, :]
        added = dot(fed, b[rows, :].astype(jnp.float32), ((0,), (0,)), precision=highest)
        last = dot(
            log_s[rows, :],
            jnp.ones((TAIL, start.shape[2]), jnp.float32),
            ((0,), (0,)),
            precision=highest,
        )
        kept = jnp.exp(last)[:, None, :] * start.astype(jnp.float32)
        fin_o[k] = (kept + added.reshape(start.shape)).astype(jnp.bfloat16)
        return carry

    lax.fori_loop(0, reqs, recur, 0)

    shares[me] = dot(rows_all[0], w[...]).astype(jnp.bfloat16)
    for s in range(1, n):
        rows_copy(s).wait_recv()
        part[s] = dot(rows_all[s], w[...]).astype(jnp.bfloat16)
        part_copy(s).start()
    for s in range(1, n):
        pltpu.make_async_remote_copy(
            src_ref=part.at[s],
            dst_ref=shares.at[to_rep(s)],
            send_sem=part_ss.at[s],
            recv_sem=part_rs.at[s],
            device_id={"rep": to_rep(s)},
            device_id_type=MESH,
        ).wait_recv()
    for u in range(1, m):
        sum_copy(u).start()
    for u in range(1, m):
        sum_copy(u).wait_recv()
    columns = w.shape[1]
    for j in range(span):
        total = shares[hd * span + j].astype(jnp.float32)
        for u in range(1, m):
            total = total + sums[u, j].astype(jnp.float32)
        proj_o[:, j * columns : (j + 1) * columns] = total.astype(jnp.bfloat16)

    for s in range(1, n):
        kv_copy(s).wait_send()
        st_copy(s).wait_send()
        rows_copy(s).wait_send()
        part_copy(s).wait_send()
    for u in range(1, m):
        sum_copy(u).wait_send()


def fused(n, m, *args):
    ssd_x, gate_z, group_b, group_c, step_dt, queries, tail_kv, ckpt_state, kv_pool, w_out = args[:10]
    decay_rate, skip_d, norm_gain, owner, slot, page_table, hit_len, tail_len = args[10:]
    reqs, heads, size, state = ckpt_state.shape
    count, width = ssd_x.shape
    page_shape = (page_table.shape[1],) + kv_pool.shape[1:]
    columns = w_out.shape[1]
    bf16 = jnp.bfloat16
    smem = pl.BlockSpec(memory_space=pltpu.SMEM)
    vmem = pl.BlockSpec(memory_space=pltpu.VMEM)
    scratch = [
        pltpu.VMEM((n,) + page_shape, bf16),
        pltpu.VMEM((n,) + page_shape, bf16),
        pltpu.VMEM((n, heads, size, state), bf16),
        pltpu.VMEM((n, heads, size, state), bf16),
        pltpu.VMEM((n, count, queries.shape[1]), bf16),
        pltpu.VMEM((n, count, columns), bf16),
        pltpu.VMEM((n, count, columns), bf16),
        pltpu.VMEM((m, n // m, count, columns), bf16),
        pltpu.VMEM((count, width), jnp.float32),
        pltpu.VMEM((count, width), jnp.float32),
        pltpu.VMEM((count, heads), jnp.float32),
        pltpu.VMEM((count, width), jnp.float32),
    ] + [pltpu.SemaphoreType.DMA((k,)) for k in (n, n, n, n, n, n, n, n, m, m)]
    return pl.pallas_call(
        functools.partial(layer, n, m),
        out_shape=(
            jax.ShapeDtypeStruct((count, width), bf16),
            jax.ShapeDtypeStruct((count, n // m * columns), bf16),
            jax.ShapeDtypeStruct(ckpt_state.shape, bf16),
        ),
        in_specs=[smem] * 5 + [vmem] * 13,
        out_specs=(vmem, vmem, vmem),
        scratch_shapes=scratch,
        compiler_params=pltpu.CompilerParams(
            collective_id=0, has_side_effects=True, vmem_limit_bytes=2 * VMEM_BUDGET
        ),
    )(
        owner,
        slot,
        page_table,
        hit_len,
        tail_len,
        *args[:10],
        decay_rate.reshape(1, -1),
        skip_d.reshape(1, -1),
        norm_gain.reshape(1, -1),
    )


def plan(n, m, *args):
    ckpt_state, kv_pool, w_out, page_table = args[7], args[8], args[9], args[15]
    state_bytes = 2 * math.prod(ckpt_state.shape[1:])
    page_bytes = 2 * page_table.shape[1] * math.prod(kv_pool.shape[1:])
    row_bytes = 2 * args[0].shape[0] * (args[5].shape[1] + 3 * w_out.shape[1])
    held = 2 * (2 * ckpt_state.size + kv_pool.size + w_out.size)
    need = n * (2 * state_bytes + 2 * page_bytes + row_bytes) + held
    one_group = (
        args[6].shape[1] == 2 * DH and args[2].shape[1] == STATE and args[5].shape[1] == QH_DEV * DH
    )
    if need <= VMEM_BUDGET and one_group and n % m == 0:
        return fused(n, m, *args)
    return local(*args)


def solution(mesh):
    return jax.shard_map(
        functools.partial(plan, mesh.shape["rep"], mesh.shape["head"]),
        mesh=mesh,
        in_specs=(
            P("rep", "head"),
            P("rep", "head"),
            P("rep", "head"),
            P("rep", "head"),
            P("rep", "head"),
            P("rep", "head"),
            P("rep", "head"),
            P("rep", "head", None, None),
            P("rep", None, "head"),
            P("head", "rep"),
            P("head"),
            P("head"),
            P("head"),
            P(),
            P(),
            P(),
            P(),
            P(),
        ),
        out_specs=(P("rep", "head"), P("rep", "head"), P("rep", "head", None, None)),
        check_vma=False,
    )
```

```python
import functools
import math

import jax
import jax.numpy as jnp
from jax import lax
from jax.experimental import pallas as pl
from jax.experimental.pallas import tpu as pltpu
from jax.sharding import PartitionSpec as P

TAIL = 16
STATE = 128
QH_DEV = 8
DH = 128


highest = lax.Precision.HIGHEST


def scan_heads(signal, b_rows, c_rows, step_sizes, state_start, rates, skipping, alive):
    length = signal.shape[1]
    head_count = signal.shape[2]
    fanout = head_count // b_rows.shape[2]
    log_decay = -rates[None, None, :] * step_sizes * alive[:, :, None]
    running = jnp.cumsum(log_decay, axis=1)
    position = jnp.arange(length, dtype=jnp.int32)
    causal = (position[:, None] >= position[None, :])[None, :, :, None]
    spans = running[:, :, None, :] - running[:, None, :, :]
    decays = jnp.where(causal, jnp.exp(jnp.where(causal, spans, 0.0)), 0.0)
    intersection = jnp.einsum("ktgn,kugn->ktug", c_rows, b_rows, precision=highest)
    intersection_head = jnp.repeat(intersection, fanout, axis=3)
    weighted_dt = step_sizes * alive[:, :, None]
    mixing = decays * intersection_head * weighted_dt[:, None, :, :]
    within = jnp.einsum("ktue,kuep->ktep", mixing, signal, precision=highest)
    c_heads = jnp.repeat(c_rows, fanout, axis=2)
    b_heads = jnp.repeat(b_rows, fanout, axis=2)
    from_state = jnp.exp(running)[..., None] * jnp.einsum(
        "kten,kepn->ktep", c_heads, state_start, precision=highest
    )
    mixer = (within + from_state + skipping[None, None, :, None] * signal) * alive[:, :, None, None]
    last_cum = running[:, -1, :]
    weights_in = jnp.exp(last_cum[:, None, :] - running) * weighted_dt
    closing = jnp.exp(last_cum)[:, :, None, None] * state_start + jnp.einsum(
        "kue,kuen,kuep->kepn", weights_in, b_heads, signal, precision=highest
    )
    return (mixer, closing)


def attend(query_rows, cached, tail_rows, hit_sizes, tail_sizes, alive):
    batch = query_rows.shape[0]
    query_len = query_rows.shape[1]
    cache_len = cached.shape[1]
    scaling = 1.0 / math.sqrt(query_rows.shape[-1])
    cached_scores = (
        jnp.einsum(
            "ktaqd,kcad->ktaqc",
            query_rows,
            cached[:, :, :, 0, :],
            preferred_element_type=jnp.float32,
        )
        * scaling
    )
    tail_scores = (
        jnp.einsum(
            "ktaqd,kuad->ktaqu",
            query_rows,
            tail_rows[:, :, :, 0, :],
            preferred_element_type=jnp.float32,
        )
        * scaling
    )
    positions = jnp.arange(cache_len, dtype=jnp.int32)
    position = jnp.arange(query_len, dtype=jnp.int32)
    seen_cache = jnp.broadcast_to(
        (positions[None, :] < hit_sizes[:, None])[:, None, :], (batch, query_len, cache_len)
    )
    seen_tail = (position[None, None, :] <= position[None, :, None]) & (
        position[None, None, :] < tail_sizes[:, None, None]
    )
    visible = jnp.concatenate([seen_cache, seen_tail], axis=2)[:, :, None, None, :]
    scores = jnp.where(visible, jnp.concatenate([cached_scores, tail_scores], axis=4), -1e30)
    row_max = jnp.max(scores, axis=4, keepdims=True)
    exponent = jnp.where(visible, jnp.exp(scores - row_max), 0.0)
    weights = (exponent / jnp.sum(exponent, axis=4, keepdims=True)).astype(jnp.bfloat16)
    result = jnp.einsum(
        "ktaqc,kcad->ktaqd",
        weights[..., :cache_len],
        cached[:, :, :, 1, :],
        preferred_element_type=jnp.float32,
    )
    result = result + jnp.einsum(
        "ktaqu,kuad->ktaqd",
        weights[..., cache_len:],
        tail_rows[:, :, :, 1, :],
        preferred_element_type=jnp.float32,
    )
    return (result * alive[:, :, None, None, None]).astype(jnp.bfloat16)


def spread(selector, values):
    flat = values.reshape(values.shape[0], -1)
    mixed = jnp.dot(selector, flat, preferred_element_type=jnp.float32)
    return mixed.astype(values.dtype).reshape((selector.shape[0],) + values.shape[1:])


def local(
    ssd_x,
    gate_z,
    group_b,
    group_c,
    step_dt,
    queries,
    tail_kv,
    ckpt_state,
    kv_pool,
    w_out,
    decay_rate,
    skip_d,
    norm_gain,
    owner,
    slot,
    page_table,
    hit_len,
    tail_len,
):
    replicas = lax.axis_size("rep")
    myself = lax.axis_index("rep")
    slot_count = ckpt_state.shape[0]
    head_count = ckpt_state.shape[1]
    head_size = ckpt_state.shape[2]
    group_width = head_count * head_size
    kv_columns = tail_kv.shape[1]
    kv_heads = kv_columns // (2 * DH)
    homes = jnp.arange(replicas, dtype=jnp.int32)
    slot_range = jnp.arange(slot_count, dtype=jnp.int32)
    owner_grid = owner.reshape(replicas, slot_count)
    slot_grid = slot.reshape(replicas, slot_count)
    hit_grid = hit_len.reshape(replicas, slot_count)
    tail_grid = tail_len.reshape(replicas, slot_count)
    page_grid = page_table.reshape(replicas, slot_count, -1)
    is_mine = (homes == myself)[:, None]
    my_owner = jnp.sum(jnp.where(is_mine, owner_grid, 0), axis=0)
    my_hit = jnp.sum(jnp.where(is_mine, hit_grid, 0), axis=0)
    my_tail = jnp.sum(jnp.where(is_mine, tail_grid, 0), axis=0)
    to_owner = (homes[:, None] == my_owner[None, :]).astype(jnp.bfloat16)
    holding = (
        (owner_grid == myself)[:, :, None] & (slot_grid[:, :, None] == slot_range[None, None, :])
    ).astype(jnp.int32)
    slot_home = jnp.sum(holding, axis=1).T.astype(jnp.bfloat16)
    slot_pages = jnp.sum(holding[:, :, :, None] * page_grid[:, :, None, :], axis=(0, 1))
    pool_range = jnp.arange(kv_pool.shape[0], dtype=jnp.int32)
    page_pick = (slot_pages.reshape(-1, 1) == pool_range[None, :]).astype(jnp.bfloat16)
    cache_own = spread(page_pick, kv_pool).reshape(slot_count, -1, kv_columns)

    def per_request(array):
        return array.reshape(slot_count, TAIL, -1)

    home_pick = slot_home.T
    fetched = (
        lax.all_to_all(
            spread(home_pick, ckpt_state), "rep", split_axis=0, concat_axis=0, tiled=True
        ),
        lax.all_to_all(
            spread(home_pick, cache_own), "rep", split_axis=0, concat_axis=0, tiled=True
        ),
    )
    owner_pick = to_owner.T
    state_start = spread(owner_pick, fetched[0])
    cached = spread(owner_pick, fetched[1])
    signal_in = per_request(ssd_x)
    batch = signal_in.shape[0]
    alive = (jnp.arange(TAIL, dtype=jnp.int32)[None, :] < my_tail[:, None]).astype(jnp.float32)
    signal = signal_in.reshape(batch, TAIL, head_count, head_size).astype(jnp.float32)
    b_rows = per_request(group_b).reshape(batch, TAIL, -1, STATE).astype(jnp.float32)
    c_rows = per_request(group_c).reshape(batch, TAIL, -1, STATE).astype(jnp.float32)
    mixer, closing = scan_heads(
        signal,
        b_rows,
        c_rows,
        per_request(step_dt).astype(jnp.float32),
        state_start.astype(jnp.float32),
        decay_rate,
        skip_d,
        alive,
    )
    gated_out = mixer * jax.nn.silu(
        per_request(gate_z).reshape(batch, TAIL, head_count, head_size).astype(jnp.float32)
    )
    energy = jnp.sum(gated_out * gated_out, axis=(2, 3))
    normed = (
        gated_out
        / jnp.sqrt(energy / group_width + 1e-05)[:, :, None, None]
        * norm_gain.reshape(head_count, head_size)
    )
    query_rows = per_request(queries).reshape(batch, TAIL, kv_heads, QH_DEV, DH)
    cached_rows = cached.reshape(batch, -1, kv_heads, 2, DH)
    tail_rows = per_request(tail_kv).reshape(batch, TAIL, kv_heads, 2, DH)
    attention = attend(query_rows, cached_rows, tail_rows, my_hit, my_tail, alive)
    ssd_rows = normed.astype(jnp.bfloat16).reshape(batch, TAIL, -1)
    attn_rows = attention.reshape(batch, TAIL, -1)
    final_rows = closing.astype(jnp.bfloat16)
    attn_flat = attn_rows.reshape(slot_count * TAIL, -1)
    terms = jnp.dot(
        attn_flat,
        lax.all_gather(w_out, "rep", axis=1, tiled=True),
        preferred_element_type=jnp.float32,
    )
    projected = lax.psum_scatter(terms, "head", scatter_dimension=1, tiled=True).astype(
        jnp.bfloat16
    )
    return (ssd_rows.reshape(slot_count * TAIL, -1), projected, final_rows)


MESH = pl.DeviceIdType.MESH
VMEM_BUDGET = 24 * 2**20


def dot(a, b, dims=((1,), (0,)), precision=None):
    return lax.dot_general(
        a, b, (dims, ((), ())), precision=precision, preferred_element_type=jnp.float32
    )


def layer(
    n,
    m,
    owner_h,
    slot_h,
    page_h,
    hit_h,
    tail_h,
    x_h,
    z_h,
    b_h,
    c_h,
    dt_h,
    q_h,
    tkv_h,
    ckpt_h,
    pool_h,
    w_h,
    rate_h,
    skip_h,
    gain_h,
    ssd_o,
    proj_o,
    fin_o,
    owner,
    slot,
    page,
    hit,
    tail,
    x,
    z,
    b,
    c,
    dt,
    q,
    tkv,
    ckpt,
    pool,
    w,
    rate,
    skip,
    gain,
    kv_out,
    kv_in,
    st_out,
    st_in,
    rows_all,
    part,
    shares,
    sums,
    cum_s,
    xw_s,
    log_s,
    acc_s,
    kv_ss,
    kv_rs,
    st_ss,
    st_rs,
    rows_ss,
    rows_rs,
    part_ss,
    part_rs,
    sum_ss,
    sum_rs,
    in_sem,
    w_ss,
    w_rs,
):
    me = lax.axis_index("rep")
    hd = lax.axis_index("head")
    reqs = ckpt.shape[0]
    heads = ckpt.shape[1]
    size = ckpt.shape[2]
    width = heads * size
    pages = page.shape[1]
    cache = pages * pool.shape[1]
    span = n // m
    chips = n // 2
    core = lax.rem(me, 2)
    twin = me + 1 - 2 * core
    chip_first = me - core
    sources = (owner_h, slot_h, page_h, hit_h, tail_h, pool_h, ckpt_h, dt_h, rate_h, skip_h)
    sources += (x_h, b_h, c_h, q_h, tkv_h, z_h, gain_h, w_h)
    targets = (owner, slot, page, hit, tail, pool, ckpt, dt, rate, skip)
    targets += (x, b, c, q, tkv, z, gain, w.at[core])
    loads = [
        pltpu.make_async_copy(source, target, in_sem.at[i])
        for i, (source, target) in enumerate(zip(sources, targets))
    ]
    for load in loads:
        load.start()

    def to_rep(s):
        return lax.rem(me + s, n)

    def from_rep(s):
        return lax.rem(me + n - s, n)

    barrier = pltpu.get_barrier_semaphore()
    for s in range(1, n):
        pl.semaphore_signal(
            barrier, inc=1, device_id={"rep": to_rep(s)}, device_id_type=MESH
        )
    for u in range(1, m):
        pl.semaphore_signal(
            barrier, inc=1, device_id={"head": lax.rem(hd + u, m)}, device_id_type=MESH
        )

    def kv_copy(s):
        return pltpu.make_async_remote_copy(
            src_ref=kv_out.at[s],
            dst_ref=kv_in.at[s],
            send_sem=kv_ss.at[s],
            recv_sem=kv_rs.at[s],
            device_id={"rep": to_rep(s)},
            device_id_type=MESH,
        )

    def st_copy(s):
        return pltpu.make_async_remote_copy(
            src_ref=st_out.at[s],
            dst_ref=st_in.at[s],
            send_sem=st_ss.at[s],
            recv_sem=st_rs.at[s],
            device_id={"rep": to_rep(s)},
            device_id_type=MESH,
        )

    def w_copy():
        return pltpu.make_async_remote_copy(
            src_ref=w_h,
            dst_ref=w.at[core],
            send_sem=w_ss,
            recv_sem=w_rs,
            device_id={"rep": twin},
            device_id_type=MESH,
        )

    def rows_copy(s):
        return pltpu.make_async_remote_copy(
            src_ref=rows_all.at[0],
            dst_ref=rows_all.at[s],
            send_sem=rows_ss.at[s],
            recv_sem=rows_rs.at[s],
            device_id={"rep": to_rep(2 * s)},
            device_id_type=MESH,
        )

    def part_copy(s):
        return pltpu.make_async_remote_copy(
            src_ref=part.at[s],
            dst_ref=shares.at[pl.ds(chip_first, 2)],
            send_sem=part_ss.at[s],
            recv_sem=part_rs.at[s],
            device_id={"rep": from_rep(2 * s)},
            device_id_type=MESH,
        )

    def sum_copy(u):
        to = lax.rem(hd + u, m)
        return pltpu.make_async_remote_copy(
            src_ref=shares.at[pl.ds(to * span, span)],
            dst_ref=sums.at[u],
            send_sem=sum_ss.at[u],
            recv_sem=sum_rs.at[u],
            device_id={"head": to},
            device_id_type=MESH,
        )

    def wanted(j):
        request = j * reqs
        for k in range(1, reqs):
            request = jnp.where(owner[j * reqs + k] == me, j * reqs + k, request)
        return request

    def pack_pages(s, target):
        request = wanted(to_rep(s))

        def one(i, carry):
            target[s, i] = pool[page[request, i]]
            return carry

        lax.fori_loop(0, pages, one, 0)

    for load in loads[:6]:
        load.wait()
    for s in range(1, n):
        pack_pages(s, kv_out)
        if s == 1:
            pl.semaphore_wait(barrier, n - 1 + m - 1)
        kv_copy(s).start()
    pack_pages(0, kv_in)

    def pack_state(s, target):
        place = slot[wanted(to_rep(s))]

        def one(e, carry):
            target[s, e] = ckpt[place, e]
            return carry

        lax.fori_loop(0, heads, one, 0)

    early = chips - 1
    loads[6].wait()
    for s in range(1, early + 1):
        pack_state(s, st_out)
        st_copy(s).start()
    w_copy().start()
    pack_state(0, st_in)
    for s in range(early + 1, n):
        pack_state(s, st_out)
    for load in loads[7:]:
        load.wait()

    lane = lax.broadcasted_iota(jnp.int32, (heads, width), 1)
    widen = (lane // size == lax.broadcasted_iota(jnp.int32, (heads, width), 0)).astype(
        jnp.float32
    )
    count = reqs * TAIL
    row = lax.broadcasted_iota(jnp.int32, (count, heads), 0)
    live = jnp.zeros((count, heads), jnp.float32)
    for k in range(reqs):
        first = k * TAIL
        live = jnp.where((row >= first) & (row < first + tail[me * reqs + k]), 1.0, live)
    weighted = dt[...].astype(jnp.float32) * live
    log_decay = -rate[...] * weighted
    log_s[...] = log_decay
    one_row = lax.broadcasted_iota(jnp.int32, (count, count), 0)
    one_col = lax.broadcasted_iota(jnp.int32, (count, count), 1)
    before = ((one_row >= one_col) & (one_row // TAIL == one_col // TAIL)).astype(jnp.float32)
    cum = dot(before, log_decay, precision=highest)
    cum_s[...] = dot(cum, widen, precision=highest)
    xw_s[...] = dot(weighted, widen, precision=highest) * x[...].astype(jnp.float32)
    skip_wide = dot(skip[...], widen, precision=highest)
    step = lax.broadcasted_iota(jnp.int32, (TAIL, 1), 0)

    def within(k, carry):
        rows = pl.ds(pl.multiple_of(k * TAIL, TAIL), TAIL)
        meet = dot(c[rows, :], b[rows, :], ((1,), (1,)))
        running = cum_s[rows, :]
        fed = xw_s[rows, :]
        total = skip_wide * x[rows, :].astype(jnp.float32)
        for u in range(TAIL):
            seen = step >= u
            decay = jnp.exp(jnp.where(seen, running - running[u : u + 1, :], 0.0))
            factor = jnp.where(seen, meet[:, u : u + 1], 0.0)
            total = total + decay * factor * fed[u : u + 1, :]
        acc_s[rows, :] = total
        return carry

    lax.fori_loop(0, reqs, within, 0)

    for s in range(1, n):
        kv_copy(s).wait_recv()

    scaling = 1.0 / math.sqrt(DH)

    def attention(k, carry):
        rows = pl.ds(pl.multiple_of(k * TAIL, TAIL), TAIL)
        request = me * reqs + k
        held = kv_in[lax.rem(me + n - owner[request], n)].reshape(cache, 2 * DH)
        fresh = tkv[rows, :]
        asked = jnp.concatenate(
            [q[rows, a * DH : (a + 1) * DH] for a in range(QH_DEV)], axis=0
        )
        far = dot(asked, held[:, :DH], ((1,), (1,))) * scaling
        near = dot(asked, fresh[:, :DH], ((1,), (1,))) * scaling
        place = lax.broadcasted_iota(jnp.int32, far.shape, 1)
        far_seen = place < hit[request]
        at = lax.rem(lax.broadcasted_iota(jnp.int32, near.shape, 0), TAIL)
        behind = lax.broadcasted_iota(jnp.int32, near.shape, 1)
        near_seen = (behind <= at) & (behind < tail[request])
        far = jnp.where(far_seen, far, -1e30)
        near = jnp.where(near_seen, near, -1e30)
        top = jnp.maximum(
            jnp.max(far, axis=1, keepdims=True), jnp.max(near, axis=1, keepdims=True)
        )
        far = jnp.where(far_seen, jnp.exp(far - top), 0.0)
        near = jnp.where(near_seen, jnp.exp(near - top), 0.0)
        whole = jnp.sum(far, axis=1, keepdims=True) + jnp.sum(near, axis=1, keepdims=True)
        far = (far / whole).astype(jnp.bfloat16)
        near = (near / whole).astype(jnp.bfloat16)
        result = dot(far, held[:, DH:]) + dot(near, fresh[:, DH:])
        result = jnp.concatenate(
            [result[a * TAIL : (a + 1) * TAIL, :] for a in range(QH_DEV)], axis=1
        )
        alive = (step < tail[request]).astype(jnp.float32)
        rows_all[0, rows, :] = (result * alive).astype(jnp.bfloat16)
        return carry

    lax.fori_loop(0, reqs, attention, 0)
    for s in range(1, chips):
        rows_copy(s).start()
    for s in range(early + 1, n):
        st_copy(s).start()

    def recur(k, carry):
        rows = pl.ds(pl.multiple_of(k * TAIL, TAIL), TAIL)
        request = me * reqs + k
        start = st_in[lax.rem(me + n - owner[request], n)]
        running = cum_s[rows, :]
        carried = dot(c[rows, :], start.reshape(width, start.shape[2]), ((1,), (1,)))
        alive = (step < tail[request]).astype(jnp.float32)
        mixer = (acc_s[rows, :] + jnp.exp(running) * carried) * alive
        gate = z[rows, :].astype(jnp.float32)
        gated = mixer * (gate / (1.0 + jnp.exp(-gate)))
        energy = jnp.sum(gated * gated, axis=1, keepdims=True)
        normed = gated / jnp.sqrt(energy / width + 1e-05) * gain[...]
        ssd_o[rows, :] = normed.astype(jnp.bfloat16)
        fed = jnp.exp(running[TAIL - 1 : TAIL, :] - running) * xw_s[rows, :]
        added = dot(fed, b[rows, :].astype(jnp.float32), ((0,), (0,)), precision=highest)
        last = dot(
            log_s[rows, :],
            jnp.ones((TAIL, start.shape[2]), jnp.float32),
            ((0,), (0,)),
            precision=highest,
        )
        kept = jnp.exp(last)[:, None, :] * start.astype(jnp.float32)
        fin_o[k] = (kept + added.reshape(start.shape)).astype(jnp.bfloat16)
        return carry

    pltpu.make_async_remote_copy(
        src_ref=w_h,
        dst_ref=w.at[1 - core],
        send_sem=w_ss,
        recv_sem=w_rs,
        device_id={"rep": twin},
        device_id_type=MESH,
    ).wait_recv()
    for i in range(2):
        shares[chip_first + i] = dot(rows_all[0], w[i]).astype(jnp.bfloat16)
    for s in range(1, chips):
        rows_copy(s).wait_recv()
        for i in range(2):
            part[s, i] = dot(rows_all[s], w[i]).astype(jnp.bfloat16)
        part_copy(s).start()
    for s in range(1, chips):
        peer = to_rep(2 * s)
        pltpu.make_async_remote_copy(
            src_ref=part.at[s],
            dst_ref=shares.at[pl.ds(peer - core, 2)],
            send_sem=part_ss.at[s],
            recv_sem=part_rs.at[s],
            device_id={"rep": peer},
            device_id_type=MESH,
        ).wait_recv()
    for u in range(1, m):
        sum_copy(u).start()

    for s in range(1, n):
        st_copy(s).wait_recv()
    lax.fori_loop(0, reqs, recur, 0)

    for u in range(1, m):
        sum_copy(u).wait_recv()
    columns = w.shape[2]
    for j in range(span):
        total = shares[hd * span + j].astype(jnp.float32)
        for u in range(1, m):
            total = total + sums[u, j].astype(jnp.float32)
        proj_o[:, j * columns : (j + 1) * columns] = total.astype(jnp.bfloat16)

    for s in range(1, n):
        kv_copy(s).wait_send()
        st_copy(s).wait_send()
    for s in range(1, chips):
        rows_copy(s).wait_send()
        part_copy(s).wait_send()
    w_copy().wait_send()
    for u in range(1, m):
        sum_copy(u).wait_send()


def fused(n, m, *args):
    ssd_x, gate_z, group_b, group_c, step_dt, queries, tail_kv, ckpt_state, kv_pool, w_out = args[:10]
    decay_rate, skip_d, norm_gain, owner, slot, page_table, hit_len, tail_len = args[10:]
    reqs, heads, size, state = ckpt_state.shape
    count, width = ssd_x.shape
    page_shape = (page_table.shape[1],) + kv_pool.shape[1:]
    columns = w_out.shape[1]
    bf16 = jnp.bfloat16
    hbm = pl.BlockSpec(memory_space=pltpu.HBM)
    vmem = pl.BlockSpec(memory_space=pltpu.VMEM)
    params = [p.reshape(1, -1) for p in (decay_rate, skip_d, norm_gain)]
    operands = (owner, slot, page_table, hit_len, tail_len, *args[:10], *params)
    scratch = [pltpu.SMEM(p.shape, p.dtype) for p in operands[:5]]
    scratch += [pltpu.VMEM(p.shape, p.dtype) for p in operands[5:14]]
    scratch += [pltpu.VMEM((2,) + w_out.shape, bf16)]
    scratch += [pltpu.VMEM(p.shape, p.dtype) for p in params]
    scratch += [
        pltpu.VMEM((n,) + page_shape, bf16),
        pltpu.VMEM((n,) + page_shape, bf16),
        pltpu.VMEM((n, heads, size, state), bf16),
        pltpu.VMEM((n, heads, size, state), bf16),
        pltpu.VMEM((n // 2, count, queries.shape[1]), bf16),
        pltpu.VMEM((n // 2, 2, count, columns), bf16),
        pltpu.VMEM((n, count, columns), bf16),
        pltpu.VMEM((m, n // m, count, columns), bf16),
        pltpu.VMEM((count, width), jnp.float32),
        pltpu.VMEM((count, width), jnp.float32),
        pltpu.VMEM((count, heads), jnp.float32),
        pltpu.VMEM((count, width), jnp.float32),
    ] + [pltpu.SemaphoreType.DMA((k,)) for k in (n, n, n, n, n, n, n, n, m, m, 18)]
    scratch += [pltpu.SemaphoreType.DMA, pltpu.SemaphoreType.DMA]
    return pl.pallas_call(
        functools.partial(layer, n, m),
        out_shape=(
            jax.ShapeDtypeStruct((count, width), bf16),
            jax.ShapeDtypeStruct((count, n // m * columns), bf16),
            jax.ShapeDtypeStruct(ckpt_state.shape, bf16),
        ),
        in_specs=[hbm] * 18,
        out_specs=(vmem, vmem, vmem),
        scratch_shapes=scratch,
        compiler_params=pltpu.CompilerParams(
            collective_id=0, has_side_effects=True, vmem_limit_bytes=2 * VMEM_BUDGET
        ),
    )(*operands)


def plan(n, m, *args):
    ckpt_state, kv_pool, w_out, page_table = args[7], args[8], args[9], args[15]
    state_bytes = 2 * math.prod(ckpt_state.shape[1:])
    page_bytes = 2 * page_table.shape[1] * math.prod(kv_pool.shape[1:])
    row_bytes = 2 * args[0].shape[0] * (args[5].shape[1] + 3 * w_out.shape[1])
    held = 2 * (2 * ckpt_state.size + kv_pool.size + 2 * w_out.size)
    need = n * (2 * state_bytes + 2 * page_bytes + row_bytes) + held
    one_group = (
        args[6].shape[1] == 2 * DH and args[2].shape[1] == STATE and args[5].shape[1] == QH_DEV * DH
    )
    if need <= VMEM_BUDGET and one_group and n % m == 0 and n % 2 == 0:
        return fused(n, m, *args)
    return local(*args)


def solution(mesh):
    return jax.shard_map(
        functools.partial(plan, mesh.shape["rep"], mesh.shape["head"]),
        mesh=mesh,
        in_specs=(
            P("rep", "head"),
            P("rep", "head"),
            P("rep", "head"),
            P("rep", "head"),
            P("rep", "head"),
            P("rep", "head"),
            P("rep", "head"),
            P("rep", "head", None, None),
            P("rep", None, "head"),
            P("head", "rep"),
            P("head"),
            P("head"),
            P("head"),
            P(),
            P(),
            P(),
            P(),
            P(),
        ),
        out_specs=(P("rep", "head"), P("rep", "head"), P("rep", "head", None, None)),
        check_vma=False,
    )
```

```python
import functools
import itertools
import math

import jax
import jax.numpy as jnp
from jax import lax
from jax.experimental import pallas as pl
from jax.experimental.pallas import tpu as pltpu
from jax.sharding import PartitionSpec as P

TAIL = 16
STATE = 128
QH_DEV = 8
DH = 128


highest = lax.Precision.HIGHEST


def scan_heads(signal, b_rows, c_rows, step_sizes, state_start, rates, skipping, alive):
    length = signal.shape[1]
    head_count = signal.shape[2]
    fanout = head_count // b_rows.shape[2]
    log_decay = -rates[None, None, :] * step_sizes * alive[:, :, None]
    running = jnp.cumsum(log_decay, axis=1)
    position = jnp.arange(length, dtype=jnp.int32)
    causal = (position[:, None] >= position[None, :])[None, :, :, None]
    spans = running[:, :, None, :] - running[:, None, :, :]
    decays = jnp.where(causal, jnp.exp(jnp.where(causal, spans, 0.0)), 0.0)
    intersection = jnp.einsum("ktgn,kugn->ktug", c_rows, b_rows, precision=highest)
    intersection_head = jnp.repeat(intersection, fanout, axis=3)
    weighted_dt = step_sizes * alive[:, :, None]
    mixing = decays * intersection_head * weighted_dt[:, None, :, :]
    within = jnp.einsum("ktue,kuep->ktep", mixing, signal, precision=highest)
    c_heads = jnp.repeat(c_rows, fanout, axis=2)
    b_heads = jnp.repeat(b_rows, fanout, axis=2)
    from_state = jnp.exp(running)[..., None] * jnp.einsum(
        "kten,kepn->ktep", c_heads, state_start, precision=highest
    )
    mixer = (within + from_state + skipping[None, None, :, None] * signal) * alive[:, :, None, None]
    last_cum = running[:, -1, :]
    weights_in = jnp.exp(last_cum[:, None, :] - running) * weighted_dt
    closing = jnp.exp(last_cum)[:, :, None, None] * state_start + jnp.einsum(
        "kue,kuen,kuep->kepn", weights_in, b_heads, signal, precision=highest
    )
    return (mixer, closing)


def attend(query_rows, cached, tail_rows, hit_sizes, tail_sizes, alive):
    batch = query_rows.shape[0]
    query_len = query_rows.shape[1]
    cache_len = cached.shape[1]
    scaling = 1.0 / math.sqrt(query_rows.shape[-1])
    cached_scores = (
        jnp.einsum(
            "ktaqd,kcad->ktaqc",
            query_rows,
            cached[:, :, :, 0, :],
            preferred_element_type=jnp.float32,
        )
        * scaling
    )
    tail_scores = (
        jnp.einsum(
            "ktaqd,kuad->ktaqu",
            query_rows,
            tail_rows[:, :, :, 0, :],
            preferred_element_type=jnp.float32,
        )
        * scaling
    )
    positions = jnp.arange(cache_len, dtype=jnp.int32)
    position = jnp.arange(query_len, dtype=jnp.int32)
    seen_cache = jnp.broadcast_to(
        (positions[None, :] < hit_sizes[:, None])[:, None, :], (batch, query_len, cache_len)
    )
    seen_tail = (position[None, None, :] <= position[None, :, None]) & (
        position[None, None, :] < tail_sizes[:, None, None]
    )
    visible = jnp.concatenate([seen_cache, seen_tail], axis=2)[:, :, None, None, :]
    scores = jnp.where(visible, jnp.concatenate([cached_scores, tail_scores], axis=4), -1e30)
    row_max = jnp.max(scores, axis=4, keepdims=True)
    exponent = jnp.where(visible, jnp.exp(scores - row_max), 0.0)
    weights = (exponent / jnp.sum(exponent, axis=4, keepdims=True)).astype(jnp.bfloat16)
    result = jnp.einsum(
        "ktaqc,kcad->ktaqd",
        weights[..., :cache_len],
        cached[:, :, :, 1, :],
        preferred_element_type=jnp.float32,
    )
    result = result + jnp.einsum(
        "ktaqu,kuad->ktaqd",
        weights[..., cache_len:],
        tail_rows[:, :, :, 1, :],
        preferred_element_type=jnp.float32,
    )
    return (result * alive[:, :, None, None, None]).astype(jnp.bfloat16)


def spread(selector, values):
    flat = values.reshape(values.shape[0], -1)
    mixed = jnp.dot(selector, flat, preferred_element_type=jnp.float32)
    return mixed.astype(values.dtype).reshape((selector.shape[0],) + values.shape[1:])


def local(
    ssd_x,
    gate_z,
    group_b,
    group_c,
    step_dt,
    queries,
    tail_kv,
    ckpt_state,
    kv_pool,
    w_out,
    decay_rate,
    skip_d,
    norm_gain,
    owner,
    slot,
    page_table,
    hit_len,
    tail_len,
):
    replicas = lax.axis_size("rep")
    myself = lax.axis_index("rep")
    slot_count = ckpt_state.shape[0]
    head_count = ckpt_state.shape[1]
    head_size = ckpt_state.shape[2]
    group_width = head_count * head_size
    kv_columns = tail_kv.shape[1]
    kv_heads = kv_columns // (2 * DH)
    homes = jnp.arange(replicas, dtype=jnp.int32)
    slot_range = jnp.arange(slot_count, dtype=jnp.int32)
    owner_grid = owner.reshape(replicas, slot_count)
    slot_grid = slot.reshape(replicas, slot_count)
    hit_grid = hit_len.reshape(replicas, slot_count)
    tail_grid = tail_len.reshape(replicas, slot_count)
    page_grid = page_table.reshape(replicas, slot_count, -1)
    is_mine = (homes == myself)[:, None]
    my_owner = jnp.sum(jnp.where(is_mine, owner_grid, 0), axis=0)
    my_hit = jnp.sum(jnp.where(is_mine, hit_grid, 0), axis=0)
    my_tail = jnp.sum(jnp.where(is_mine, tail_grid, 0), axis=0)
    to_owner = (homes[:, None] == my_owner[None, :]).astype(jnp.bfloat16)
    holding = (
        (owner_grid == myself)[:, :, None] & (slot_grid[:, :, None] == slot_range[None, None, :])
    ).astype(jnp.int32)
    slot_home = jnp.sum(holding, axis=1).T.astype(jnp.bfloat16)
    slot_pages = jnp.sum(holding[:, :, :, None] * page_grid[:, :, None, :], axis=(0, 1))
    pool_range = jnp.arange(kv_pool.shape[0], dtype=jnp.int32)
    page_pick = (slot_pages.reshape(-1, 1) == pool_range[None, :]).astype(jnp.bfloat16)
    cache_own = spread(page_pick, kv_pool).reshape(slot_count, -1, kv_columns)

    def per_request(array):
        return array.reshape(slot_count, TAIL, -1)

    home_pick = slot_home.T
    fetched = (
        lax.all_to_all(
            spread(home_pick, ckpt_state), "rep", split_axis=0, concat_axis=0, tiled=True
        ),
        lax.all_to_all(
            spread(home_pick, cache_own), "rep", split_axis=0, concat_axis=0, tiled=True
        ),
    )
    owner_pick = to_owner.T
    state_start = spread(owner_pick, fetched[0])
    cached = spread(owner_pick, fetched[1])
    signal_in = per_request(ssd_x)
    batch = signal_in.shape[0]
    alive = (jnp.arange(TAIL, dtype=jnp.int32)[None, :] < my_tail[:, None]).astype(jnp.float32)
    signal = signal_in.reshape(batch, TAIL, head_count, head_size).astype(jnp.float32)
    b_rows = per_request(group_b).reshape(batch, TAIL, -1, STATE).astype(jnp.float32)
    c_rows = per_request(group_c).reshape(batch, TAIL, -1, STATE).astype(jnp.float32)
    mixer, closing = scan_heads(
        signal,
        b_rows,
        c_rows,
        per_request(step_dt).astype(jnp.float32),
        state_start.astype(jnp.float32),
        decay_rate,
        skip_d,
        alive,
    )
    gated_out = mixer * jax.nn.silu(
        per_request(gate_z).reshape(batch, TAIL, head_count, head_size).astype(jnp.float32)
    )
    energy = jnp.sum(gated_out * gated_out, axis=(2, 3))
    normed = (
        gated_out
        / jnp.sqrt(energy / group_width + 1e-05)[:, :, None, None]
        * norm_gain.reshape(head_count, head_size)
    )
    query_rows = per_request(queries).reshape(batch, TAIL, kv_heads, QH_DEV, DH)
    cached_rows = cached.reshape(batch, -1, kv_heads, 2, DH)
    tail_rows = per_request(tail_kv).reshape(batch, TAIL, kv_heads, 2, DH)
    attention = attend(query_rows, cached_rows, tail_rows, my_hit, my_tail, alive)
    ssd_rows = normed.astype(jnp.bfloat16).reshape(batch, TAIL, -1)
    attn_rows = attention.reshape(batch, TAIL, -1)
    final_rows = closing.astype(jnp.bfloat16)
    attn_flat = attn_rows.reshape(slot_count * TAIL, -1)
    terms = jnp.dot(
        attn_flat,
        lax.all_gather(w_out, "rep", axis=1, tiled=True),
        preferred_element_type=jnp.float32,
    )
    projected = lax.psum_scatter(terms, "head", scatter_dimension=1, tiled=True).astype(
        jnp.bfloat16
    )
    return (ssd_rows.reshape(slot_count * TAIL, -1), projected, final_rows)


MESH = pl.DeviceIdType.MESH
VMEM_BUDGET = 24 * 2**20
SHARES = (1, 2, 2, 2)
VMEM_LIMIT = 62 * 2**20


def dot(a, b, dims=((1,), (0,)), precision=None):
    return lax.dot_general(
        a, b, (dims, ((), ())), precision=precision, preferred_element_type=jnp.float32
    )


def layer(
    n,
    m,
    owner_h,
    slot_h,
    page_h,
    hit_h,
    tail_h,
    x_h,
    z_h,
    b_h,
    c_h,
    dt_h,
    q_h,
    tkv_h,
    ckpt_h,
    pool_h,
    w_h,
    rate_h,
    skip_h,
    gain_h,
    ssd_o,
    proj_o,
    fin_o,
    owner,
    slot,
    page,
    hit,
    tail,
    x,
    z,
    b,
    c,
    dt,
    q,
    tkv,
    ckpt,
    pool,
    w,
    rate,
    skip,
    gain,
    kv_out,
    kv_in,
    st_out,
    st_in,
    rows_all,
    part,
    shares,
    sums,
    cum_s,
    xw_s,
    log_s,
    acc_s,
    kv_ss,
    kv_rs,
    st_ss,
    st_rs,
    rows_ss,
    rows_rs,
    part_ss,
    part_rs,
    sum_ss,
    sum_rs,
    in_sem,
    w_ss,
    w_rs,
):
    me = lax.axis_index("rep")
    hd = lax.axis_index("head")
    reqs = ckpt.shape[0]
    heads = ckpt.shape[1]
    size = ckpt.shape[2]
    width = heads * size
    pages = page.shape[0]
    cache = pages * pool.shape[1]
    span = n // m
    chips = n // 2
    core = lax.rem(me, 2)
    twin = me + 1 - 2 * core
    chip_first = me - core
    sources = (owner_h, slot_h, page_h, hit_h, tail_h, pool_h, ckpt_h, dt_h, rate_h, skip_h)
    sources += (x_h, b_h, c_h, q_h, tkv_h, z_h, gain_h, w_h)
    targets = (owner, slot, page, hit, tail, pool, ckpt, dt, rate, skip)
    targets += (x, b, c, q, tkv, z, gain, w.at[core])
    loads = [
        pltpu.make_async_copy(source, target, in_sem.at[i])
        for i, (source, target) in enumerate(zip(sources, targets))
    ]
    for load in loads:
        load.start()

    def to_rep(s):
        return lax.rem(me + s, n)

    def from_rep(s):
        return lax.rem(me + n - s, n)

    barrier = pltpu.get_barrier_semaphore()
    for s in range(1, n):
        pl.semaphore_signal(
            barrier, inc=1, device_id={"rep": to_rep(s)}, device_id_type=MESH
        )
    for u in range(1, m):
        pl.semaphore_signal(
            barrier, inc=1, device_id={"head": lax.rem(hd + u, m)}, device_id_type=MESH
        )

    def kv_copy(s):
        return pltpu.make_async_remote_copy(
            src_ref=kv_out.at[s],
            dst_ref=kv_in.at[s],
            send_sem=kv_ss.at[s],
            recv_sem=kv_rs.at[s],
            device_id={"rep": to_rep(s)},
            device_id_type=MESH,
        )

    def st_copy(s):
        return pltpu.make_async_remote_copy(
            src_ref=st_out.at[s],
            dst_ref=st_in.at[s],
            send_sem=st_ss.at[s],
            recv_sem=st_rs.at[s],
            device_id={"rep": to_rep(s)},
            device_id_type=MESH,
        )

    def w_copy():
        return pltpu.make_async_remote_copy(
            src_ref=w_h,
            dst_ref=w.at[core],
            send_sem=w_ss,
            recv_sem=w_rs,
            device_id={"rep": twin},
            device_id_type=MESH,
        )

    def rows_copy(s):
        return pltpu.make_async_remote_copy(
            src_ref=rows_all.at[0],
            dst_ref=rows_all.at[s],
            send_sem=rows_ss.at[s],
            recv_sem=rows_rs.at[s],
            device_id={"rep": to_rep(2 * s)},
            device_id_type=MESH,
        )

    def part_copy(s):
        return pltpu.make_async_remote_copy(
            src_ref=part.at[s],
            dst_ref=shares.at[pl.ds(chip_first, 2)],
            send_sem=part_ss.at[s],
            recv_sem=part_rs.at[s],
            device_id={"rep": from_rep(2 * s)},
            device_id_type=MESH,
        )

    def sum_copy(u):
        to = lax.rem(hd + u, m)
        return pltpu.make_async_remote_copy(
            src_ref=shares.at[pl.ds(to * span, span)],
            dst_ref=sums.at[u],
            send_sem=sum_ss.at[u],
            recv_sem=sum_rs.at[u],
            device_id={"head": to},
            device_id_type=MESH,
        )

    def wanted(j):
        request = j * reqs
        for k in range(1, reqs):
            request = jnp.where(owner[j * reqs + k] == me, j * reqs + k, request)
        return request

    def pack_pages(s, target):
        request = wanted(to_rep(s))

        def one(i, carry):
            target[s, i] = pool[page[i, request]]
            return carry

        lax.fori_loop(0, pages, one, 0)

    for load in loads[:6]:
        load.wait()
    for s in range(1, n):
        pack_pages(s, kv_out)
        if s == 1:
            pl.semaphore_wait(barrier, n - 1 + m - 1)
        kv_copy(s).start()
    pack_pages(0, kv_in)

    def pack_state(s, target):
        place = slot[wanted(to_rep(s))]

        def one(e, carry):
            target[s, e] = ckpt[place, e]
            return carry

        lax.fori_loop(0, heads, one, 0)

    stops = [(n - 1) * k // sum(SHARES) for k in itertools.accumulate(SHARES)]
    first, second, third, fourth = (
        range(1 + begin, 1 + end) for begin, end in zip([0] + stops, stops)
    )
    loads[6].wait()
    for s in first:
        pack_state(s, st_out)
        st_copy(s).start()
    w_copy().start()
    pack_state(0, st_in)
    for s in range(1 + stops[0], n):
        pack_state(s, st_out)
    for load in loads[7:]:
        load.wait()

    lane = lax.broadcasted_iota(jnp.int32, (heads, width), 1)
    widen = (lane // size == lax.broadcasted_iota(jnp.int32, (heads, width), 0)).astype(
        jnp.float32
    )
    count = reqs * TAIL
    row = lax.broadcasted_iota(jnp.int32, (count, heads), 0)
    live = jnp.zeros((count, heads), jnp.float32)
    for k in range(reqs):
        first = k * TAIL
        live = jnp.where((row >= first) & (row < first + tail[me * reqs + k]), 1.0, live)
    same = lax.broadcasted_iota(jnp.int32, (heads, heads), 0) == lax.broadcasted_iota(
        jnp.int32, (heads, heads), 1
    )
    steps = dot(dt[...].astype(jnp.float32), same.astype(jnp.float32), ((0,), (0,)), highest)
    weighted = steps * live
    log_decay = -rate[...] * weighted
    log_s[...] = log_decay
    one_row = lax.broadcasted_iota(jnp.int32, (count, count), 0)
    one_col = lax.broadcasted_iota(jnp.int32, (count, count), 1)
    before = ((one_row >= one_col) & (one_row // TAIL == one_col // TAIL)).astype(jnp.float32)
    cum = dot(before, log_decay, precision=highest)
    cum_s[...] = dot(cum, widen, precision=highest)
    xw_s[...] = dot(weighted, widen, precision=highest) * x[...].astype(jnp.float32)
    skip_wide = dot(skip[...], widen, precision=highest)
    step = lax.broadcasted_iota(jnp.int32, (TAIL, 1), 0)

    def within(k, carry):
        rows = pl.ds(pl.multiple_of(k * TAIL, TAIL), TAIL)
        meet = dot(c[rows, :], b[rows, :], ((1,), (1,)))
        running = cum_s[rows, :]
        fed = xw_s[rows, :]
        total = skip_wide * x[rows, :].astype(jnp.float32)
        for u in range(TAIL):
            seen = step >= u
            decay = jnp.exp(jnp.where(seen, running - running[u : u + 1, :], 0.0))
            factor = jnp.where(seen, meet[:, u : u + 1], 0.0)
            total = total + decay * factor * fed[u : u + 1, :]
        acc_s[rows, :] = total
        return carry

    lax.fori_loop(0, reqs, within, 0)

    for s in range(1, n):
        kv_copy(s).wait_recv()

    scaling = 1.0 / math.sqrt(DH)

    def attention(k, carry):
        rows = pl.ds(pl.multiple_of(k * TAIL, TAIL), TAIL)
        request = me * reqs + k
        held = kv_in[lax.rem(me + n - owner[request], n)].reshape(cache, 2 * DH)
        fresh = tkv[rows, :]
        asked = jnp.concatenate(
            [q[rows, a * DH : (a + 1) * DH] for a in range(QH_DEV)], axis=0
        )
        far = dot(asked, held[:, :DH], ((1,), (1,))) * scaling
        near = dot(asked, fresh[:, :DH], ((1,), (1,))) * scaling
        place = lax.broadcasted_iota(jnp.int32, far.shape, 1)
        far_seen = place < hit[request]
        at = lax.rem(lax.broadcasted_iota(jnp.int32, near.shape, 0), TAIL)
        behind = lax.broadcasted_iota(jnp.int32, near.shape, 1)
        near_seen = (behind <= at) & (behind < tail[request])
        far = jnp.where(far_seen, far, -1e30)
        near = jnp.where(near_seen, near, -1e30)
        top = jnp.maximum(
            jnp.max(far, axis=1, keepdims=True), jnp.max(near, axis=1, keepdims=True)
        )
        far = jnp.where(far_seen, jnp.exp(far - top), 0.0)
        near = jnp.where(near_seen, jnp.exp(near - top), 0.0)
        whole = jnp.sum(far, axis=1, keepdims=True) + jnp.sum(near, axis=1, keepdims=True)
        far = (far / whole).astype(jnp.bfloat16)
        near = (near / whole).astype(jnp.bfloat16)
        result = dot(far, held[:, DH:]) + dot(near, fresh[:, DH:])
        result = jnp.concatenate(
            [result[a * TAIL : (a + 1) * TAIL, :] for a in range(QH_DEV)], axis=1
        )
        alive = (step < tail[request]).astype(jnp.float32)
        rows_all[0, rows, :] = (result * alive).astype(jnp.bfloat16)
        return carry

    lax.fori_loop(0, reqs, attention, 0)
    for s in range(1, chips):
        rows_copy(s).start()
    for s in second:
        st_copy(s).start()

    def recur(k, carry):
        rows = pl.ds(pl.multiple_of(k * TAIL, TAIL), TAIL)
        request = me * reqs + k
        start = st_in[lax.rem(me + n - owner[request], n)]
        running = cum_s[rows, :]
        carried = dot(c[rows, :], start.reshape(width, start.shape[2]), ((1,), (1,)))
        alive = (step < tail[request]).astype(jnp.float32)
        mixer = (acc_s[rows, :] + jnp.exp(running) * carried) * alive
        gate = z[rows, :].astype(jnp.float32)
        gated = mixer * (gate / (1.0 + jnp.exp(-gate)))
        energy = jnp.sum(gated * gated, axis=1, keepdims=True)
        normed = gated / jnp.sqrt(energy / width + 1e-05) * gain[...]
        ssd_o[rows, :] = normed.astype(jnp.bfloat16)
        fed = jnp.exp(running[TAIL - 1 : TAIL, :] - running) * xw_s[rows, :]
        added = dot(fed, b[rows, :].astype(jnp.float32), ((0,), (0,)), precision=highest)
        last = dot(
            log_s[rows, :],
            jnp.ones((TAIL, start.shape[2]), jnp.float32),
            ((0,), (0,)),
            precision=highest,
        )
        kept = jnp.exp(last)[:, None, :] * start.astype(jnp.float32)
        fin_o[k] = (kept + added.reshape(start.shape)).astype(jnp.bfloat16)
        return carry

    pltpu.make_async_remote_copy(
        src_ref=w_h,
        dst_ref=w.at[1 - core],
        send_sem=w_ss,
        recv_sem=w_rs,
        device_id={"rep": twin},
        device_id_type=MESH,
    ).wait_recv()
    for i in range(2):
        shares[chip_first + i] = dot(rows_all[0], w[i]).astype(jnp.bfloat16)
    for s in range(1, chips):
        rows_copy(s).wait_recv()
        for i in range(2):
            part[s, i] = dot(rows_all[s], w[i]).astype(jnp.bfloat16)
        part_copy(s).start()
    for s in third:
        st_copy(s).start()
    for s in range(1, chips):
        peer = to_rep(2 * s)
        pltpu.make_async_remote_copy(
            src_ref=part.at[s],
            dst_ref=shares.at[pl.ds(peer - core, 2)],
            send_sem=part_ss.at[s],
            recv_sem=part_rs.at[s],
            device_id={"rep": peer},
            device_id_type=MESH,
        ).wait_recv()
    for u in range(1, m):
        sum_copy(u).start()
    for s in fourth:
        st_copy(s).start()

    for s in range(1, n):
        st_copy(s).wait_recv()
    lax.fori_loop(0, reqs, recur, 0)

    for u in range(1, m):
        sum_copy(u).wait_recv()
    columns = w.shape[2]
    for j in range(span):
        total = shares[hd * span + j].astype(jnp.float32)
        for u in range(1, m):
            total = total + sums[u, j].astype(jnp.float32)
        proj_o[:, j * columns : (j + 1) * columns] = total.astype(jnp.bfloat16)

    for s in range(1, n):
        kv_copy(s).wait_send()
        st_copy(s).wait_send()
    for s in range(1, chips):
        rows_copy(s).wait_send()
        part_copy(s).wait_send()
    w_copy().wait_send()
    for u in range(1, m):
        sum_copy(u).wait_send()


def fused(n, m, *args):
    ssd_x, gate_z, group_b, group_c, step_dt, queries, tail_kv, ckpt_state, kv_pool, w_out = args[:10]
    decay_rate, skip_d, norm_gain, owner, slot, page_table, hit_len, tail_len = args[10:]
    reqs, heads, size, state = ckpt_state.shape
    count, width = ssd_x.shape
    page_shape = (page_table.shape[1],) + kv_pool.shape[1:]
    columns = w_out.shape[1]
    bf16 = jnp.bfloat16
    hbm = pl.BlockSpec(memory_space=pltpu.HBM)
    vmem = pl.BlockSpec(memory_space=pltpu.VMEM)
    params = [p.reshape(1, -1) for p in (decay_rate, skip_d, norm_gain)]
    operands = (owner, slot, page_table.T, hit_len, tail_len)
    operands += (*args[:4], step_dt.T, *args[5:10], *params)
    scratch = [pltpu.SMEM(p.shape, p.dtype) for p in operands[:5]]
    scratch += [pltpu.VMEM(p.shape, p.dtype) for p in operands[5:14]]
    scratch += [pltpu.VMEM((2,) + w_out.shape, bf16)]
    scratch += [pltpu.VMEM(p.shape, p.dtype) for p in params]
    scratch += [
        pltpu.VMEM((n,) + page_shape, bf16),
        pltpu.VMEM((n,) + page_shape, bf16),
        pltpu.VMEM((n, heads, size, state), bf16),
        pltpu.VMEM((n, heads, size, state), bf16),
        pltpu.VMEM((n // 2, count, queries.shape[1]), bf16),
        pltpu.VMEM((n // 2, 2, count, columns), bf16),
        pltpu.VMEM((n, count, columns), bf16),
        pltpu.VMEM((m, n // m, count, columns), bf16),
        pltpu.VMEM((count, width), jnp.float32),
        pltpu.VMEM((count, width), jnp.float32),
        pltpu.VMEM((count, heads), jnp.float32),
        pltpu.VMEM((count, width), jnp.float32),
    ] + [pltpu.SemaphoreType.DMA((k,)) for k in (n, n, n, n, n, n, n, n, m, m, 18)]
    scratch += [pltpu.SemaphoreType.DMA, pltpu.SemaphoreType.DMA]
    return pl.pallas_call(
        functools.partial(layer, n, m),
        out_shape=(
            jax.ShapeDtypeStruct((count, width), bf16),
            jax.ShapeDtypeStruct((count, n // m * columns), bf16),
            jax.ShapeDtypeStruct(ckpt_state.shape, bf16),
        ),
        in_specs=[hbm] * 18,
        out_specs=(vmem, vmem, vmem),
        scratch_shapes=scratch,
        compiler_params=pltpu.CompilerParams(
            collective_id=0, has_side_effects=True, vmem_limit_bytes=VMEM_LIMIT
        ),
    )(*operands)


def plan(n, m, *args):
    ckpt_state, kv_pool, w_out, page_table = args[7], args[8], args[9], args[15]
    state_bytes = 2 * math.prod(ckpt_state.shape[1:])
    page_bytes = 2 * page_table.shape[1] * math.prod(kv_pool.shape[1:])
    row_bytes = 2 * args[0].shape[0] * (args[5].shape[1] + 3 * w_out.shape[1])
    held = 2 * (2 * ckpt_state.size + kv_pool.size + 2 * w_out.size)
    need = n * (2 * state_bytes + 2 * page_bytes + row_bytes) + held
    one_group = (
        args[6].shape[1] == 2 * DH and args[2].shape[1] == STATE and args[5].shape[1] == QH_DEV * DH
    )
    if need <= VMEM_BUDGET and one_group and n % m == 0 and n % 2 == 0:
        return fused(n, m, *args)
    return local(*args)


def solution(mesh):
    return jax.shard_map(
        functools.partial(plan, mesh.shape["rep"], mesh.shape["head"]),
        mesh=mesh,
        in_specs=(
            P("rep", "head"),
            P("rep", "head"),
            P("rep", "head"),
            P("rep", "head"),
            P("rep", "head"),
            P("rep", "head"),
            P("rep", "head"),
            P("rep", "head", None, None),
            P("rep", None, "head"),
            P("head", "rep"),
            P("head"),
            P("head"),
            P("head"),
            P(),
            P(),
            P(),
            P(),
            P(),
        ),
        out_specs=(P("rep", "head"), P("rep", "head"), P("rep", "head", None, None)),
        check_vma=False,
    )
```

```python
import functools
import itertools
import math

import jax
import jax.numpy as jnp
from jax import lax
from jax.experimental import pallas as pl
from jax.experimental.pallas import tpu as pltpu
from jax.sharding import PartitionSpec as P

TAIL = 16
STATE = 128
QH_DEV = 8
DH = 128


highest = lax.Precision.HIGHEST


def scan_heads(signal, b_rows, c_rows, step_sizes, state_start, rates, skipping, alive):
    length = signal.shape[1]
    head_count = signal.shape[2]
    fanout = head_count // b_rows.shape[2]
    log_decay = -rates[None, None, :] * step_sizes * alive[:, :, None]
    running = jnp.cumsum(log_decay, axis=1)
    position = jnp.arange(length, dtype=jnp.int32)
    causal = (position[:, None] >= position[None, :])[None, :, :, None]
    spans = running[:, :, None, :] - running[:, None, :, :]
    decays = jnp.where(causal, jnp.exp(jnp.where(causal, spans, 0.0)), 0.0)
    intersection = jnp.einsum("ktgn,kugn->ktug", c_rows, b_rows, precision=highest)
    intersection_head = jnp.repeat(intersection, fanout, axis=3)
    weighted_dt = step_sizes * alive[:, :, None]
    mixing = decays * intersection_head * weighted_dt[:, None, :, :]
    within = jnp.einsum("ktue,kuep->ktep", mixing, signal, precision=highest)
    c_heads = jnp.repeat(c_rows, fanout, axis=2)
    b_heads = jnp.repeat(b_rows, fanout, axis=2)
    from_state = jnp.exp(running)[..., None] * jnp.einsum(
        "kten,kepn->ktep", c_heads, state_start, precision=highest
    )
    mixer = (within + from_state + skipping[None, None, :, None] * signal) * alive[:, :, None, None]
    last_cum = running[:, -1, :]
    weights_in = jnp.exp(last_cum[:, None, :] - running) * weighted_dt
    closing = jnp.exp(last_cum)[:, :, None, None] * state_start + jnp.einsum(
        "kue,kuen,kuep->kepn", weights_in, b_heads, signal, precision=highest
    )
    return (mixer, closing)


def attend(query_rows, cached, tail_rows, hit_sizes, tail_sizes, alive):
    batch = query_rows.shape[0]
    query_len = query_rows.shape[1]
    cache_len = cached.shape[1]
    scaling = 1.0 / math.sqrt(query_rows.shape[-1])
    cached_scores = (
        jnp.einsum(
            "ktaqd,kcad->ktaqc",
            query_rows,
            cached[:, :, :, 0, :],
            preferred_element_type=jnp.float32,
        )
        * scaling
    )
    tail_scores = (
        jnp.einsum(
            "ktaqd,kuad->ktaqu",
            query_rows,
            tail_rows[:, :, :, 0, :],
            preferred_element_type=jnp.float32,
        )
        * scaling
    )
    positions = jnp.arange(cache_len, dtype=jnp.int32)
    position = jnp.arange(query_len, dtype=jnp.int32)
    seen_cache = jnp.broadcast_to(
        (positions[None, :] < hit_sizes[:, None])[:, None, :], (batch, query_len, cache_len)
    )
    seen_tail = (position[None, None, :] <= position[None, :, None]) & (
        position[None, None, :] < tail_sizes[:, None, None]
    )
    visible = jnp.concatenate([seen_cache, seen_tail], axis=2)[:, :, None, None, :]
    scores = jnp.where(visible, jnp.concatenate([cached_scores, tail_scores], axis=4), -1e30)
    row_max = jnp.max(scores, axis=4, keepdims=True)
    exponent = jnp.where(visible, jnp.exp(scores - row_max), 0.0)
    weights = (exponent / jnp.sum(exponent, axis=4, keepdims=True)).astype(jnp.bfloat16)
    result = jnp.einsum(
        "ktaqc,kcad->ktaqd",
        weights[..., :cache_len],
        cached[:, :, :, 1, :],
        preferred_element_type=jnp.float32,
    )
    result = result + jnp.einsum(
        "ktaqu,kuad->ktaqd",
        weights[..., cache_len:],
        tail_rows[:, :, :, 1, :],
        preferred_element_type=jnp.float32,
    )
    return (result * alive[:, :, None, None, None]).astype(jnp.bfloat16)


def spread(selector, values):
    flat = values.reshape(values.shape[0], -1)
    mixed = jnp.dot(selector, flat, preferred_element_type=jnp.float32)
    return mixed.astype(values.dtype).reshape((selector.shape[0],) + values.shape[1:])


def local(
    ssd_x,
    gate_z,
    group_b,
    group_c,
    step_dt,
    queries,
    tail_kv,
    ckpt_state,
    kv_pool,
    w_out,
    decay_rate,
    skip_d,
    norm_gain,
    owner,
    slot,
    page_table,
    hit_len,
    tail_len,
):
    replicas = lax.axis_size("rep")
    myself = lax.axis_index("rep")
    slot_count = ckpt_state.shape[0]
    head_count = ckpt_state.shape[1]
    head_size = ckpt_state.shape[2]
    group_width = head_count * head_size
    kv_columns = tail_kv.shape[1]
    kv_heads = kv_columns // (2 * DH)
    homes = jnp.arange(replicas, dtype=jnp.int32)
    slot_range = jnp.arange(slot_count, dtype=jnp.int32)
    owner_grid = owner.reshape(replicas, slot_count)
    slot_grid = slot.reshape(replicas, slot_count)
    hit_grid = hit_len.reshape(replicas, slot_count)
    tail_grid = tail_len.reshape(replicas, slot_count)
    page_grid = page_table.reshape(replicas, slot_count, -1)
    is_mine = (homes == myself)[:, None]
    my_owner = jnp.sum(jnp.where(is_mine, owner_grid, 0), axis=0)
    my_hit = jnp.sum(jnp.where(is_mine, hit_grid, 0), axis=0)
    my_tail = jnp.sum(jnp.where(is_mine, tail_grid, 0), axis=0)
    to_owner = (homes[:, None] == my_owner[None, :]).astype(jnp.bfloat16)
    holding = (
        (owner_grid == myself)[:, :, None] & (slot_grid[:, :, None] == slot_range[None, None, :])
    ).astype(jnp.int32)
    slot_home = jnp.sum(holding, axis=1).T.astype(jnp.bfloat16)
    slot_pages = jnp.sum(holding[:, :, :, None] * page_grid[:, :, None, :], axis=(0, 1))
    pool_range = jnp.arange(kv_pool.shape[0], dtype=jnp.int32)
    page_pick = (slot_pages.reshape(-1, 1) == pool_range[None, :]).astype(jnp.bfloat16)
    cache_own = spread(page_pick, kv_pool).reshape(slot_count, -1, kv_columns)

    def per_request(array):
        return array.reshape(slot_count, TAIL, -1)

    home_pick = slot_home.T
    fetched = (
        lax.all_to_all(
            spread(home_pick, ckpt_state), "rep", split_axis=0, concat_axis=0, tiled=True
        ),
        lax.all_to_all(
            spread(home_pick, cache_own), "rep", split_axis=0, concat_axis=0, tiled=True
        ),
    )
    owner_pick = to_owner.T
    state_start = spread(owner_pick, fetched[0])
    cached = spread(owner_pick, fetched[1])
    signal_in = per_request(ssd_x)
    batch = signal_in.shape[0]
    alive = (jnp.arange(TAIL, dtype=jnp.int32)[None, :] < my_tail[:, None]).astype(jnp.float32)
    signal = signal_in.reshape(batch, TAIL, head_count, head_size).astype(jnp.float32)
    b_rows = per_request(group_b).reshape(batch, TAIL, -1, STATE).astype(jnp.float32)
    c_rows = per_request(group_c).reshape(batch, TAIL, -1, STATE).astype(jnp.float32)
    mixer, closing = scan_heads(
        signal,
        b_rows,
        c_rows,
        per_request(step_dt).astype(jnp.float32),
        state_start.astype(jnp.float32),
        decay_rate,
        skip_d,
        alive,
    )
    gated_out = mixer * jax.nn.silu(
        per_request(gate_z).reshape(batch, TAIL, head_count, head_size).astype(jnp.float32)
    )
    energy = jnp.sum(gated_out * gated_out, axis=(2, 3))
    normed = (
        gated_out
        / jnp.sqrt(energy / group_width + 1e-05)[:, :, None, None]
        * norm_gain.reshape(head_count, head_size)
    )
    query_rows = per_request(queries).reshape(batch, TAIL, kv_heads, QH_DEV, DH)
    cached_rows = cached.reshape(batch, -1, kv_heads, 2, DH)
    tail_rows = per_request(tail_kv).reshape(batch, TAIL, kv_heads, 2, DH)
    attention = attend(query_rows, cached_rows, tail_rows, my_hit, my_tail, alive)
    ssd_rows = normed.astype(jnp.bfloat16).reshape(batch, TAIL, -1)
    attn_rows = attention.reshape(batch, TAIL, -1)
    final_rows = closing.astype(jnp.bfloat16)
    attn_flat = attn_rows.reshape(slot_count * TAIL, -1)
    terms = jnp.dot(
        attn_flat,
        lax.all_gather(w_out, "rep", axis=1, tiled=True),
        preferred_element_type=jnp.float32,
    )
    projected = lax.psum_scatter(terms, "head", scatter_dimension=1, tiled=True).astype(
        jnp.bfloat16
    )
    return (ssd_rows.reshape(slot_count * TAIL, -1), projected, final_rows)


MESH = pl.DeviceIdType.MESH
VMEM_BUDGET = 24 * 2**20
SHARES = (1, 2, 2, 2)
VMEM_LIMIT = 62 * 2**20


def dot(a, b, dims=((1,), (0,)), precision=None):
    return lax.dot_general(
        a, b, (dims, ((), ())), precision=precision, preferred_element_type=jnp.float32
    )


def layer(
    n,
    m,
    owner_h,
    slot_h,
    page_h,
    hit_h,
    tail_h,
    x_h,
    z_h,
    b_h,
    c_h,
    dt_h,
    q_h,
    tkv_h,
    ckpt_h,
    pool_h,
    w_h,
    rate_h,
    skip_h,
    gain_h,
    ssd_o,
    proj_o,
    fin_o,
    owner,
    slot,
    page,
    hit,
    tail,
    x,
    z,
    b,
    c,
    dt,
    q,
    tkv,
    ckpt,
    pool,
    w,
    rate,
    skip,
    gain,
    kv_out,
    kv_in,
    st_out,
    st_in,
    rows_all,
    part,
    shares,
    sums,
    cum_s,
    xw_s,
    log_s,
    acc_s,
    add_s,
    keep_s,
    kv_ss,
    kv_rs,
    st_ss,
    st_rs,
    rows_ss,
    rows_rs,
    part_ss,
    part_rs,
    sum_ss,
    sum_rs,
    in_sem,
    w_ss,
    w_rs,
):
    me = lax.axis_index("rep")
    hd = lax.axis_index("head")
    reqs = ckpt.shape[0]
    heads = ckpt.shape[1]
    size = ckpt.shape[2]
    width = heads * size
    pages = page.shape[0]
    cache = pages * pool.shape[1]
    span = n // m
    chips = n // 2
    core = lax.rem(me, 2)
    twin = me + 1 - 2 * core
    chip_first = me - core
    sources = (owner_h, slot_h, page_h, hit_h, tail_h, pool_h, ckpt_h, dt_h, rate_h, skip_h)
    sources += (x_h, b_h, c_h, q_h, tkv_h, z_h, gain_h, w_h)
    targets = (owner, slot, page, hit, tail, pool, ckpt, dt, rate, skip)
    targets += (x, b, c, q, tkv, z, gain, w.at[core])
    loads = [
        pltpu.make_async_copy(source, target, in_sem.at[i])
        for i, (source, target) in enumerate(zip(sources, targets))
    ]
    for load in loads:
        load.start()

    def to_rep(s):
        return lax.rem(me + s, n)

    def from_rep(s):
        return lax.rem(me + n - s, n)

    barrier = pltpu.get_barrier_semaphore()
    for s in range(1, n):
        pl.semaphore_signal(
            barrier, inc=1, device_id={"rep": to_rep(s)}, device_id_type=MESH
        )
    for u in range(1, m):
        pl.semaphore_signal(
            barrier, inc=1, device_id={"head": lax.rem(hd + u, m)}, device_id_type=MESH
        )

    def kv_copy(s):
        return pltpu.make_async_remote_copy(
            src_ref=kv_out.at[s],
            dst_ref=kv_in.at[s],
            send_sem=kv_ss.at[s],
            recv_sem=kv_rs.at[s],
            device_id={"rep": to_rep(s)},
            device_id_type=MESH,
        )

    def st_copy(s):
        return pltpu.make_async_remote_copy(
            src_ref=st_out.at[s],
            dst_ref=st_in.at[s],
            send_sem=st_ss.at[s],
            recv_sem=st_rs.at[s],
            device_id={"rep": to_rep(s)},
            device_id_type=MESH,
        )

    def w_copy():
        return pltpu.make_async_remote_copy(
            src_ref=w_h,
            dst_ref=w.at[core],
            send_sem=w_ss,
            recv_sem=w_rs,
            device_id={"rep": twin},
            device_id_type=MESH,
        )

    def rows_copy(s):
        return pltpu.make_async_remote_copy(
            src_ref=rows_all.at[0],
            dst_ref=rows_all.at[s],
            send_sem=rows_ss.at[s],
            recv_sem=rows_rs.at[s],
            device_id={"rep": to_rep(2 * s)},
            device_id_type=MESH,
        )

    def part_copy(s):
        return pltpu.make_async_remote_copy(
            src_ref=part.at[s],
            dst_ref=shares.at[pl.ds(chip_first, 2)],
            send_sem=part_ss.at[s],
            recv_sem=part_rs.at[s],
            device_id={"rep": from_rep(2 * s)},
            device_id_type=MESH,
        )

    def sum_copy(u):
        to = lax.rem(hd + u, m)
        return pltpu.make_async_remote_copy(
            src_ref=shares.at[pl.ds(to * span, span)],
            dst_ref=sums.at[u],
            send_sem=sum_ss.at[u],
            recv_sem=sum_rs.at[u],
            device_id={"head": to},
            device_id_type=MESH,
        )

    def wanted(j):
        request = j * reqs
        for k in range(1, reqs):
            request = jnp.where(owner[j * reqs + k] == me, j * reqs + k, request)
        return request

    def pack_pages(s, target):
        request = wanted(to_rep(s))

        def one(i, carry):
            target[s, i] = pool[page[i, request]]
            return carry

        lax.fori_loop(0, pages, one, 0)

    for load in loads[:6]:
        load.wait()
    for s in range(1, n):
        pack_pages(s, kv_out)
        if s == 1:
            pl.semaphore_wait(barrier, n - 1 + m - 1)
        kv_copy(s).start()
    pack_pages(0, kv_in)

    def pack_state(s, target):
        place = slot[wanted(to_rep(s))]

        def one(e, carry):
            target[s, e] = ckpt[place, e]
            return carry

        lax.fori_loop(0, heads, one, 0)

    stops = [(n - 1) * k // sum(SHARES) for k in itertools.accumulate(SHARES)]
    first, second, third, fourth = (
        range(1 + begin, 1 + end) for begin, end in zip([0] + stops, stops)
    )
    loads[6].wait()
    for s in first:
        pack_state(s, st_out)
        st_copy(s).start()
    w_copy().start()
    pack_state(0, st_in)
    for s in range(1 + stops[0], n):
        pack_state(s, st_out)
    for load in loads[7:]:
        load.wait()

    lane = lax.broadcasted_iota(jnp.int32, (heads, width), 1)
    widen = (lane // size == lax.broadcasted_iota(jnp.int32, (heads, width), 0)).astype(
        jnp.float32
    )
    count = reqs * TAIL
    row = lax.broadcasted_iota(jnp.int32, (count, heads), 0)
    live = jnp.zeros((count, heads), jnp.float32)
    for k in range(reqs):
        first = k * TAIL
        live = jnp.where((row >= first) & (row < first + tail[me * reqs + k]), 1.0, live)
    same = lax.broadcasted_iota(jnp.int32, (heads, heads), 0) == lax.broadcasted_iota(
        jnp.int32, (heads, heads), 1
    )
    steps = dot(dt[...].astype(jnp.float32), same.astype(jnp.float32), ((0,), (0,)), highest)
    weighted = steps * live
    log_decay = -rate[...] * weighted
    log_s[...] = log_decay
    one_row = lax.broadcasted_iota(jnp.int32, (count, count), 0)
    one_col = lax.broadcasted_iota(jnp.int32, (count, count), 1)
    before = ((one_row >= one_col) & (one_row // TAIL == one_col // TAIL)).astype(jnp.float32)
    cum = dot(before, log_decay, precision=highest)
    cum_s[...] = dot(cum, widen, precision=highest)
    xw_s[...] = dot(weighted, widen, precision=highest) * x[...].astype(jnp.float32)
    skip_wide = dot(skip[...], widen, precision=highest)
    step = lax.broadcasted_iota(jnp.int32, (TAIL, 1), 0)

    def within(k, carry):
        rows = pl.ds(pl.multiple_of(k * TAIL, TAIL), TAIL)
        meet = dot(c[rows, :], b[rows, :], ((1,), (1,)))
        running = cum_s[rows, :]
        fed = xw_s[rows, :]
        total = skip_wide * x[rows, :].astype(jnp.float32)
        for u in range(TAIL):
            seen = step >= u
            decay = jnp.exp(jnp.where(seen, running - running[u : u + 1, :], 0.0))
            factor = jnp.where(seen, meet[:, u : u + 1], 0.0)
            total = total + decay * factor * fed[u : u + 1, :]
        acc_s[rows, :] = total
        late = jnp.exp(running[TAIL - 1 : TAIL, :] - running) * fed
        added = dot(late, b[rows, :].astype(jnp.float32), ((0,), (0,)), precision=highest)
        add_s[k] = added.reshape(add_s.shape[1:])
        last = dot(
            log_s[rows, :],
            jnp.ones((TAIL, b.shape[1]), jnp.float32),
            ((0,), (0,)),
            precision=highest,
        )
        keep_s[k] = jnp.exp(last)
        return carry

    lax.fori_loop(0, reqs, within, 0)

    for s in range(1, n):
        kv_copy(s).wait_recv()

    scaling = 1.0 / math.sqrt(DH)

    def attention(k, carry):
        rows = pl.ds(pl.multiple_of(k * TAIL, TAIL), TAIL)
        request = me * reqs + k
        held = kv_in[lax.rem(me + n - owner[request], n)].reshape(cache, 2 * DH)
        fresh = tkv[rows, :]
        asked = jnp.concatenate(
            [q[rows, a * DH : (a + 1) * DH] for a in range(QH_DEV)], axis=0
        )
        far = dot(asked, held[:, :DH], ((1,), (1,))) * scaling
        near = dot(asked, fresh[:, :DH], ((1,), (1,))) * scaling
        place = lax.broadcasted_iota(jnp.int32, far.shape, 1)
        far_seen = place < hit[request]
        at = lax.rem(lax.broadcasted_iota(jnp.int32, near.shape, 0), TAIL)
        behind = lax.broadcasted_iota(jnp.int32, near.shape, 1)
        near_seen = (behind <= at) & (behind < tail[request])
        far = jnp.where(far_seen, far, -1e30)
        near = jnp.where(near_seen, near, -1e30)
        top = jnp.maximum(
            jnp.max(far, axis=1, keepdims=True), jnp.max(near, axis=1, keepdims=True)
        )
        far = jnp.where(far_seen, jnp.exp(far - top), 0.0)
        near = jnp.where(near_seen, jnp.exp(near - top), 0.0)
        whole = jnp.sum(far, axis=1, keepdims=True) + jnp.sum(near, axis=1, keepdims=True)
        far = (far / whole).astype(jnp.bfloat16)
        near = (near / whole).astype(jnp.bfloat16)
        result = dot(far, held[:, DH:]) + dot(near, fresh[:, DH:])
        result = jnp.concatenate(
            [result[a * TAIL : (a + 1) * TAIL, :] for a in range(QH_DEV)], axis=1
        )
        alive = (step < tail[request]).astype(jnp.float32)
        rows_all[0, rows, :] = (result * alive).astype(jnp.bfloat16)
        return carry

    lax.fori_loop(0, reqs, attention, 0)
    for s in range(1, chips):
        rows_copy(s).start()
    for s in second:
        st_copy(s).start()

    def recur(k, carry):
        rows = pl.ds(pl.multiple_of(k * TAIL, TAIL), TAIL)
        request = me * reqs + k
        start = st_in[lax.rem(me + n - owner[request], n)]
        running = cum_s[rows, :]
        carried = dot(c[rows, :], start.reshape(width, start.shape[2]), ((1,), (1,)))
        alive = (step < tail[request]).astype(jnp.float32)
        mixer = (acc_s[rows, :] + jnp.exp(running) * carried) * alive
        gate = z[rows, :].astype(jnp.float32)
        gated = mixer * (gate / (1.0 + jnp.exp(-gate)))
        energy = jnp.sum(gated * gated, axis=1, keepdims=True)
        normed = gated / jnp.sqrt(energy / width + 1e-05) * gain[...]
        ssd_o[rows, :] = normed.astype(jnp.bfloat16)
        kept = keep_s[k][:, None, :] * start.astype(jnp.float32)
        fin_o[k] = (kept + add_s[k]).astype(jnp.bfloat16)
        return carry

    pltpu.make_async_remote_copy(
        src_ref=w_h,
        dst_ref=w.at[1 - core],
        send_sem=w_ss,
        recv_sem=w_rs,
        device_id={"rep": twin},
        device_id_type=MESH,
    ).wait_recv()
    for i in range(2):
        shares[chip_first + i] = dot(rows_all[0], w[i]).astype(jnp.bfloat16)
    for s in range(1, chips):
        rows_copy(s).wait_recv()
        for i in range(2):
            part[s, i] = dot(rows_all[s], w[i]).astype(jnp.bfloat16)
        part_copy(s).start()
    for s in third:
        st_copy(s).start()
    for s in range(1, chips):
        peer = to_rep(2 * s)
        pltpu.make_async_remote_copy(
            src_ref=part.at[s],
            dst_ref=shares.at[pl.ds(peer - core, 2)],
            send_sem=part_ss.at[s],
            recv_sem=part_rs.at[s],
            device_id={"rep": peer},
            device_id_type=MESH,
        ).wait_recv()
    for u in range(1, m):
        sum_copy(u).start()
    for s in fourth:
        st_copy(s).start()

    for s in range(1, n):
        st_copy(s).wait_recv()
    lax.fori_loop(0, reqs, recur, 0)

    for u in range(1, m):
        sum_copy(u).wait_recv()
    columns = w.shape[2]
    for j in range(span):
        total = shares[hd * span + j].astype(jnp.float32)
        for u in range(1, m):
            total = total + sums[u, j].astype(jnp.float32)
        proj_o[:, j * columns : (j + 1) * columns] = total.astype(jnp.bfloat16)

    for s in range(1, n):
        kv_copy(s).wait_send()
        st_copy(s).wait_send()
    for s in range(1, chips):
        rows_copy(s).wait_send()
        part_copy(s).wait_send()
    w_copy().wait_send()
    for u in range(1, m):
        sum_copy(u).wait_send()


def fused(n, m, *args):
    ssd_x, gate_z, group_b, group_c, step_dt, queries, tail_kv, ckpt_state, kv_pool, w_out = args[:10]
    decay_rate, skip_d, norm_gain, owner, slot, page_table, hit_len, tail_len = args[10:]
    reqs, heads, size, state = ckpt_state.shape
    count, width = ssd_x.shape
    page_shape = (page_table.shape[1],) + kv_pool.shape[1:]
    columns = w_out.shape[1]
    bf16 = jnp.bfloat16
    hbm = pl.BlockSpec(memory_space=pltpu.HBM)
    vmem = pl.BlockSpec(memory_space=pltpu.VMEM)
    params = [p.reshape(1, -1) for p in (decay_rate, skip_d, norm_gain)]
    operands = (owner, slot, page_table.T, hit_len, tail_len)
    operands += (*args[:4], step_dt.T, *args[5:10], *params)
    scratch = [pltpu.SMEM(p.shape, p.dtype) for p in operands[:5]]
    scratch += [pltpu.VMEM(p.shape, p.dtype) for p in operands[5:14]]
    scratch += [pltpu.VMEM((2,) + w_out.shape, bf16)]
    scratch += [pltpu.VMEM(p.shape, p.dtype) for p in params]
    scratch += [
        pltpu.VMEM((n,) + page_shape, bf16),
        pltpu.VMEM((n,) + page_shape, bf16),
        pltpu.VMEM((n, heads, size, state), bf16),
        pltpu.VMEM((n, heads, size, state), bf16),
        pltpu.VMEM((n // 2, count, queries.shape[1]), bf16),
        pltpu.VMEM((n // 2, 2, count, columns), bf16),
        pltpu.VMEM((n, count, columns), bf16),
        pltpu.VMEM((m, n // m, count, columns), bf16),
        pltpu.VMEM((count, width), jnp.float32),
        pltpu.VMEM((count, width), jnp.float32),
        pltpu.VMEM((count, heads), jnp.float32),
        pltpu.VMEM((count, width), jnp.float32),
        pltpu.VMEM((reqs, heads, size, state), jnp.float32),
        pltpu.VMEM((reqs, heads, state), jnp.float32),
    ] + [pltpu.SemaphoreType.DMA((k,)) for k in (n, n, n, n, n, n, n, n, m, m, 18)]
    scratch += [pltpu.SemaphoreType.DMA, pltpu.SemaphoreType.DMA]
    return pl.pallas_call(
        functools.partial(layer, n, m),
        out_shape=(
            jax.ShapeDtypeStruct((count, width), bf16),
            jax.ShapeDtypeStruct((count, n // m * columns), bf16),
            jax.ShapeDtypeStruct(ckpt_state.shape, bf16),
        ),
        in_specs=[hbm] * 18,
        out_specs=(vmem, vmem, vmem),
        scratch_shapes=scratch,
        compiler_params=pltpu.CompilerParams(
            collective_id=0, has_side_effects=True, vmem_limit_bytes=VMEM_LIMIT
        ),
    )(*operands)


def plan(n, m, *args):
    ckpt_state, kv_pool, w_out, page_table = args[7], args[8], args[9], args[15]
    state_bytes = 2 * math.prod(ckpt_state.shape[1:])
    page_bytes = 2 * page_table.shape[1] * math.prod(kv_pool.shape[1:])
    row_bytes = 2 * args[0].shape[0] * (args[5].shape[1] + 3 * w_out.shape[1])
    held = 2 * (2 * ckpt_state.size + kv_pool.size + 2 * w_out.size)
    need = n * (2 * state_bytes + 2 * page_bytes + row_bytes) + held
    one_group = (
        args[6].shape[1] == 2 * DH and args[2].shape[1] == STATE and args[5].shape[1] == QH_DEV * DH
    )
    if need <= VMEM_BUDGET and one_group and n % m == 0 and n % 2 == 0:
        return fused(n, m, *args)
    return local(*args)


def solution(mesh):
    return jax.shard_map(
        functools.partial(plan, mesh.shape["rep"], mesh.shape["head"]),
        mesh=mesh,
        in_specs=(
            P("rep", "head"),
            P("rep", "head"),
            P("rep", "head"),
            P("rep", "head"),
            P("rep", "head"),
            P("rep", "head"),
            P("rep", "head"),
            P("rep", "head", None, None),
            P("rep", None, "head"),
            P("head", "rep"),
            P("head"),
            P("head"),
            P("head"),
            P(),
            P(),
            P(),
            P(),
            P(),
        ),
        out_specs=(P("rep", "head"), P("rep", "head"), P("rep", "head", None, None)),
        check_vma=False,
    )
```
